32 devices in a mesh: row: 8 (over z, x), col: 4 (over y, core).
Axes of the slice: x: 2, y: 2, z: 4, core: 2. Of those that a mesh axis runs over, the one named last changes fastest.
Arguments:
- traces: bfloat16 [32, 512, 512], P(None, 'row', 'col'), may hold values from -6 to 6
- source_pos: int32 [512], P('row'), may hold values from 0 to 4095
- receiver_pos: int32 [512], replicated, may hold values from 0 to 4095
- aperture_list: int32 [32, 256], P('row'), may hold values from 0 to 511, as said below
- band_index: int32 [4096], P('row'), may hold values from 0 to 31
- weight_tiles: bfloat16 [32, 8, 128], replicated, may hold values from -2 to 2
Outputs:
- primaries: bfloat16 [32, 512, 512], P(None, 'row', 'col')
- image: float32 [512, 4096], P('col', 'row')
The draws below stay inside these ranges and needn't reach their ends.
Inputs may be any that keep to these rules, and one draw needn't show every extreme that they name: `aperture_list`: the 256 receivers listed for one tile are distinct.
All inputs are finite; a program needn't handle non-finite values.
Results may differ from the reference program's by a relative error of at most 0.012.
Values may be sent and summed in bfloat16 or wider, within the bound.
No kernel may reach another device: no remote copies, remote signals or barrier semaphores. Data moves between devices by JAX's collectives and lax.ppermute only.
A program may use at most 64 MiB of HBM per device.

```python
import math
import jax
import jax.numpy as jnp
from jax import lax

SRC_DEV = 64
NPOS = 512
TW = 32
NFFT = 4096
NF = 4
TP = 8
IX_DEV = 512
DEPTH_BAND_CELLS = 128
NXI = 4096
NZI = 512
TX = 128
APER = 256
KT = 32
HALF = 1024
N_ROW = 8
N_COL = 4


def draw_aperture_list(key, part):
    tile_keys = jax.random.split(jax.random.fold_in(key, 11), NXI // TX)

    def one_tile(tile_key):
        return jax.random.permutation(tile_key, NPOS)[:APER]
    return jax.vmap(one_tile)(tile_keys).astype(jnp.int32)


def set_ends(array, key, smallest, largest):
    longest = array.shape.index(max(array.shape))
    spots = []
    for shift in (0, 1):
        where = [jax.random.randint(jax.random.fold_in(key, axis), (), 0, length) for axis, length in enumerate(array.shape)]
        where[longest] = (where[longest] + shift) % array.shape[longest]
        spots.append(tuple(where))
    return array.at[spots[0]].set(smallest).at[spots[1]].set(largest)


def block_scale(stream_key, dims, cuts, least, high):
    gain, own = 1.0, jax.random.fold_in(stream_key, 6)
    for axis_at, blocks in cuts:
        steps = jnp.exp(jax.random.uniform(jax.random.fold_in(own, axis_at), (blocks,), jnp.float32, least / len(cuts), high / len(cuts)))
        gain = gain * jnp.repeat(steps, dims[axis_at] // blocks).reshape([-1 if axis == axis_at else 1 for axis in range(len(dims))])
    return gain


def gaussian(key, shape, spread, reach, pieces=(), held_as=jnp.bfloat16):
    entries = spread * jax.random.normal(key, shape, jnp.float32)
    if pieces:
        entries = entries * block_scale(key, shape, pieces, -0.22, 0.18)
    return jnp.clip(entries, -reach, reach).astype(held_as)


def setup_inputs(seed: int = 0) -> dict:
    arg_keys = jax.random.split(jax.random.key(seed), 7)
    traces = gaussian(arg_keys[0], (TW, NPOS, NPOS), 1.0, 6.0, ((1, 8), (2, 4)))
    source_pos = set_ends(jax.random.randint(arg_keys[1], (NPOS,), 0, NXI), jax.random.fold_in(arg_keys[1], 1), 0, NXI - 1).astype(jnp.int32)
    receiver_pos = set_ends(jax.random.randint(arg_keys[2], (NPOS,), 0, NXI), jax.random.fold_in(arg_keys[2], 1), 0, NXI - 1).astype(jnp.int32)
    aperture_list = draw_aperture_list(jax.random.fold_in(arg_keys[6], 71), 0)
    band_index = set_ends(jax.random.randint(arg_keys[4], (NXI,), 0, KT), jax.random.fold_in(arg_keys[4], 1), 0, KT - 1).astype(jnp.int32)
    weight_tiles = gaussian(arg_keys[5], (KT, TP, DEPTH_BAND_CELLS), TP ** -0.5, 2.0)
    return dict(traces=traces, source_pos=source_pos, receiver_pos=receiver_pos, aperture_list=aperture_list, band_index=band_index, weight_tiles=weight_tiles)


def phase_tables(samples):
    freq_bins = (2 * jnp.arange(NF, dtype=jnp.int32) + 1) * (NFFT // (4 * NF))
    sample_ticks = jnp.arange(samples, dtype=jnp.int32)
    phase_turns = freq_bins[:, None] * sample_ticks[None, :] % NFFT
    phase_angle = phase_turns.astype(jnp.float32) * (2.0 * math.pi / NFFT)
    return (jnp.cos(phase_angle), jnp.sin(phase_angle))

def aperture_matrix(tile_index_lists, positions, columns, first_row, row_count, spread_len):
    tile_count, listed = tile_index_lists.shape
    col_width = columns.shape[0]
    inside = (tile_index_lists >= first_row) & (tile_index_lists < first_row + row_count)
    local_index = jnp.where(inside, tile_index_lists - first_row, row_count)
    tile_rows = jnp.broadcast_to(jnp.arange(tile_count, dtype=jnp.int32)[:, None], tile_index_lists.shape)
    member = jnp.zeros((tile_count, row_count), jnp.float32).at[tile_rows, local_index].add(1.0, mode='drop')
    widened = jnp.repeat(member.T, col_width // tile_count, axis=1)
    offset = (positions[:, None] - columns[None, :]).astype(jnp.float32) / spread_len
    taper_weight = 1.0 / (1.0 + offset * offset)
    return (widened * taper_weight * (2.0 / math.sqrt(listed))).astype(jnp.bfloat16)

def shot_weights(positions, columns, spread_len):
    offset = (positions[:, None] - columns[None, :]).astype(jnp.float32) / spread_len
    return 1.0 / (1.0 + offset * offset)

def reference(traces, source_pos, receiver_pos, aperture_list, band_index, weight_tiles):
    cosine, sine_table = phase_tables(TW)
    forward = (jnp.concatenate([cosine, -sine_table], 0) / math.sqrt(TW)).astype(jnp.bfloat16)
    inverse = jnp.concatenate([cosine, -sine_table], 0).T / math.sqrt(NF)

    def spectra_block(block_index):
        trace_block = lax.dynamic_slice_in_dim(traces, block_index * SRC_DEV, SRC_DEV, 1)
        result = jnp.dot(forward.astype(jnp.float32), trace_block.reshape(TW, SRC_DEV * NPOS).astype(jnp.float32), preferred_element_type=jnp.float32)
        return result.astype(jnp.bfloat16).reshape(2 * NF, SRC_DEV, NPOS)
    blocks_out = lax.map(spectra_block, jnp.arange(N_ROW, dtype=jnp.int32))
    spectra = jnp.moveaxis(blocks_out, 0, 1).reshape(2, NF, NPOS, NPOS)

    def predict(spectrum_pair):
        real_part = spectrum_pair[0].astype(jnp.float32)
        imag_part = spectrum_pair[1].astype(jnp.float32)
        real_real = jnp.dot(real_part, real_part, preferred_element_type=jnp.float32)
        imag_imag = jnp.dot(imag_part, imag_part, preferred_element_type=jnp.float32)
        real_imag = jnp.dot(real_part, imag_part, preferred_element_type=jnp.float32)
        imag_real = jnp.dot(imag_part, real_part, preferred_element_type=jnp.float32)
        return -jnp.stack([real_real - imag_imag, real_imag + imag_real]) / math.sqrt(NPOS)
    multiples = jnp.moveaxis(lax.map(predict, jnp.moveaxis(spectra, 1, 0)), 0, 1)

    def panel_work(block_index):
        first_shot = block_index * SRC_DEV
        trace_block = lax.dynamic_slice_in_dim(traces, first_shot, SRC_DEV, 1)
        mult_block = lax.dynamic_slice_in_dim(multiples, first_shot, SRC_DEV, 2).reshape(2 * NF, SRC_DEV * NPOS)
        wave_field = jnp.dot(inverse, mult_block, precision=lax.Precision.HIGHEST, preferred_element_type=jnp.float32)
        primary_block = (trace_block.astype(jnp.float32) - wave_field.reshape(TW, SRC_DEV, NPOS)).astype(jnp.bfloat16)
        columns = block_index * IX_DEV + jnp.arange(IX_DEV, dtype=jnp.int32)
        tile_index_lists = lax.dynamic_slice_in_dim(aperture_list, block_index * (IX_DEV // TX), IX_DEV // TX, 0)
        aperture = aperture_matrix(tile_index_lists, receiver_pos, columns, 0, NPOS, HALF)
        shot_pos = lax.dynamic_slice_in_dim(source_pos, first_shot, SRC_DEV, 0)
        stacking_weights = shot_weights(shot_pos, columns, HALF)
        stacked = jnp.dot(primary_block.reshape(TW * SRC_DEV, NPOS).astype(jnp.float32), aperture.astype(jnp.float32), preferred_element_type=jnp.float32).reshape(TW, SRC_DEV, IX_DEV)
        column_stack = (lax.optimization_barrier(jnp.sum(stacked * stacking_weights[None], axis=1)) / math.sqrt(SRC_DEV)).astype(jnp.bfloat16)
        band_rows = lax.dynamic_slice_in_dim(band_index, block_index * IX_DEV, IX_DEV, 0)
        select = band_rows[None, :] == jnp.arange(KT, dtype=jnp.int32)[:, None]
        slab_stacks = column_stack.reshape(N_COL, TP, IX_DEV)
        widened = jnp.where(select[None, :, None, :], slab_stacks[:, None], jnp.zeros((), jnp.bfloat16))
        image_panel = jnp.einsum('kz,qkx->qzx', weight_tiles.reshape(KT * TP, DEPTH_BAND_CELLS).astype(jnp.float32), widened.reshape(N_COL, KT * TP, IX_DEV).astype(jnp.float32))
        return (primary_block, image_panel.reshape(N_COL * DEPTH_BAND_CELLS, IX_DEV))
    primary_blocks, image_panels = lax.map(panel_work, jnp.arange(N_ROW, dtype=jnp.int32))
    primaries = jnp.moveaxis(primary_blocks, 0, 1).reshape(TW, NPOS, NPOS)
    image_out = jnp.moveaxis(image_panels, 0, 1).reshape(NZI, NXI)
    return (primaries, image_out)
```

```python
import functools
import math

import jax
import jax.numpy as jnp
import ml_dtypes
import numpy as np
from jax import lax
from jax.experimental import pallas as pl
from jax.experimental.pallas import tpu as pltpu
from jax.sharding import PartitionSpec as P

NFFT = 4096
NF = 4
STEP = NFFT // (4 * NF)
HALF_TURN = NFFT // (2 * STEP)
F32 = jnp.float32
BF16 = jnp.bfloat16
VMEM_BYTES = 48 * 1024 * 1024


def angle(freq, sample):
    return 2.0 * math.pi * (((2 * freq + 1) * STEP * sample) % NFFT) / NFFT


def forward_weight(freq, part, sample, samples):
    value = (math.cos, lambda a: -math.sin(a))[part](angle(freq, sample)) / math.sqrt(samples)
    return float(np.float32(value).astype(ml_dtypes.bfloat16)) if abs(value) > 1e-6 else 0.0


def weighted_sum(weights, arrays):
    total = None
    for weight, array in zip(weights, arrays):
        if abs(weight) > 1e-6:
            total = weight * array if total is None else total + weight * array
    return total


def dot(left, right):
    return jnp.dot(left, right, preferred_element_type=F32)


def member_index():
    return lax.rem(lax.axis_index("row"), NF)


def spectra_kernel(traces, held, own, send_1, send_2, send_3, planes, arrived):
    samples, shots, _ = held.shape
    rows = shots // 4
    copies = []
    for part in range(4):
        piece = (slice(None), pl.ds(part * rows, rows))
        copies.append(pltpu.make_async_copy(traces.at[piece], held.at[piece], arrived.at[part]))
        copies[-1].start()
    for part in range(4):
        copies[part].wait()
        here = slice(part * rows, (part + 1) * rows)
        folded = []
        for sample in range(HALF_TURN):
            total = held[sample, here].astype(F32)
            for turn in range(1, samples // HALF_TURN):
                term = held[sample + turn * HALF_TURN, here].astype(F32)
                total = total - term if turn % 2 else total + term
            folded.append(total)
        for freq in range(NF):
            for piece in range(2):
                weights = [forward_weight(freq, piece, t, samples) for t in range(HALF_TURN)]
                planes[freq, piece, here] = weighted_sum(weights, folded).astype(BF16)
    me = member_index()
    for offset, out in enumerate((own, send_1, send_2, send_3)):
        out[...] = planes[me ^ offset]


def rows_kernel(own, got_1, got_2, got_3, block):
    me = member_index()
    for offset, got in enumerate((own, got_1, got_2, got_3)):
        for piece in range(2):
            block[piece, me ^ offset] = got[piece]


def product_kernel(left_offsets, groups, *refs):
    n_left = len(left_offsets)
    lefts, rights = refs[:n_left], refs[n_left : n_left + groups]
    outs = refs[n_left + groups : n_left + groups + NF]
    left, right, product = refs[n_left + groups + NF :]
    me, group = member_index(), lax.axis_index("row") // NF
    col = lax.axis_index("col")
    for offset, got in zip(left_offsets, lefts):
        left[col ^ offset] = got[...]
    for offset, got in enumerate(rights):
        right[group ^ offset] = got[...]
    rows = left.shape[2] * left.shape[3]
    lanes = left.shape[4]
    ratio = n_left // groups
    total = None
    for index in range(groups):
        real, imag = (right[index, piece].reshape(rows, lanes) for piece in range(2))
        left_real, left_imag = (
            jnp.concatenate(
                [left[index * ratio + k, piece].reshape(rows, lanes) for k in range(ratio)], axis=1
            )
            for piece in range(2)
        )
        term = dot(left_real, jnp.concatenate([real, imag], axis=1))
        term = term + dot(left_imag, jnp.concatenate([-imag, real], axis=1))
        total = term if total is None else total + term
    scale = -1.0 / math.sqrt(rows * groups)
    product[...] = (total * scale).reshape(product.shape).astype(BF16)
    for offset, out in enumerate(outs):
        out[...] = product[me ^ offset]


def tables_kernel(
    spread_len, held, block, receiver_pos, aperture_list, source_pos, band_index, weight_tiles,
    aperture, shot_weight, stacked, tiles_turned, chosen,
):
    del block
    samples, shots, receivers = held.shape
    panel = aperture.shape[1]
    tiles, listed = aperture_list.shape
    width = panel // tiles
    col = lax.axis_index("col")
    first = lax.axis_index("row") * panel

    def upright(row, length):
        at_row = lax.broadcasted_iota(jnp.int32, (length, length), 0)
        at_lane = lax.broadcasted_iota(jnp.int32, (length, length), 1)
        return jnp.sum(jnp.where(at_row == at_lane, row.astype(F32), 0.0), axis=1, keepdims=True)

    def taper(positions, length):
        columns = (lax.broadcasted_iota(jnp.int32, (length, panel), 1) + first).astype(F32)
        offset = (positions - columns) / spread_len
        return 1.0 / (1.0 + offset * offset)

    position = upright(receiver_pos[pl.ds(col, 1)], receivers)
    near = taper(position, receivers)
    receiver = lax.broadcasted_iota(jnp.int32, (receivers, listed), 0) + col * receivers
    ones = jnp.ones((listed, width), BF16)
    for tile in range(tiles):
        hits = jnp.where(aperture_list[tile : tile + 1] == receiver, 1.0, 0.0).astype(BF16)
        counts = dot(hits, ones)
        here = slice(tile * width, (tile + 1) * width)
        aperture[:, here] = (counts * near[:, here] * (2.0 / math.sqrt(listed))).astype(BF16)
    shot_weight[...] = taper(upright(source_pos[...], shots), shots)
    bands, steps, _ = stacked.shape
    for band in range(bands):
        lines = []
        for step in range(steps):
            line = dot(held[band * steps + step], aperture[...])
            lines.append(jnp.sum(line * shot_weight[...], axis=0, keepdims=True))
        stacked[band] = jnp.concatenate(lines, axis=0)
    tiles_turned[...] = weight_tiles[...].astype(F32).T.astype(BF16)
    kinds = chosen.shape[0]
    kind = lax.broadcasted_iota(jnp.int32, (kinds, panel), 0)
    chosen[...] = jnp.where(band_index[...] == kind, 1.0, 0.0)


def stack_kernel(own, got_1, got_2, got_3, aperture, shot_weight, stacked, keep, send, multiples, columns):
    me, col = member_index(), lax.axis_index("col")
    for offset, got in enumerate((own, got_1, got_2, got_3)):
        multiples[me ^ offset] = got[...]
    shots, receivers = multiples.shape[1], multiples.shape[2] // 2
    lines = []
    for freq in range(NF):
        for piece in range(2):
            part = multiples[freq, :, piece * receivers : (piece + 1) * receivers]
            line = dot(part, aperture[...]) * shot_weight[...]
            lines.append(jnp.sum(line, axis=0, keepdims=True))
    waves = []
    for sample in range(HALF_TURN):
        weights = []
        for freq in range(NF):
            weights += [math.cos(angle(freq, sample)), -math.sin(angle(freq, sample))]
        waves.append(weighted_sum([w / math.sqrt(NF) for w in weights], lines))
    bands, steps, _ = stacked.shape
    for band in range(bands):
        start = band * steps
        wave = jnp.concatenate([waves[(start + k) % HALF_TURN] for k in range(steps)], axis=0)
        sign = -1.0 if (start // HALF_TURN) % 2 else 1.0
        columns[band] = stacked[band] - sign * wave
    half = keep.shape[0]
    for offset in range(half):
        keep[offset] = columns[col ^ offset]
        send[offset] = columns[col ^ (offset + half)]


def halve_kernel(kept, got, keep, send):
    half = keep.shape[0]
    for offset in range(half):
        keep[offset] = kept[offset] + got[offset]
        send[offset] = kept[offset + half] + got[offset + half]


def primaries_kernel(own, got_1, got_2, got_3, held, out, multiples):
    me = member_index()
    for offset, got in enumerate((own, got_1, got_2, got_3)):
        multiples[me ^ offset] = got[...]
    samples, shots, receivers = held.shape
    rows = 16
    for start in range(0, shots, rows):
        here = slice(start, start + rows)
        parts = []
        for freq in range(NF):
            for piece in range(2):
                lanes = slice(piece * receivers, (piece + 1) * receivers)
                parts.append(multiples[freq, here, lanes].astype(F32))
        for sample in range(HALF_TURN):
            weights = []
            for freq in range(NF):
                weights += [math.cos(angle(freq, sample)), -math.sin(angle(freq, sample))]
            wave = weighted_sum([w / math.sqrt(NF) for w in weights], parts)
            for turn in range(samples // HALF_TURN):
                at = sample + turn * HALF_TURN
                trace = held[at, here].astype(F32)
                out[at, here] = (trace + wave if turn % 2 else trace - wave).astype(BF16)


def image_kernel(shots, kept, got, tiles_turned, chosen, primaries, image):
    del primaries
    column_stack = (kept[0] + got[0]) / math.sqrt(shots)
    steps, panel = column_stack.shape
    kinds = chosen.shape[0]
    rounded = column_stack.astype(BF16).astype(F32)
    widened = jnp.where(chosen[...][:, None, :] > 0.5, rounded[None], 0.0)
    image[...] = dot(tiles_turned[...], widened.reshape(kinds * steps, panel).astype(BF16))


WHOLE = pl.BlockSpec(memory_space=pltpu.VMEM)
ANYWHERE = pl.BlockSpec(memory_space=pl.ANY)


def in_vmem(*arrays):
    return [pltpu.with_memory_space_constraint(a, pltpu.VMEM) for a in arrays]


def call(body, out_shape, in_specs, out_specs, scratch=(), flops=0, moved=0):
    return pl.pallas_call(
        body,
        out_shape=out_shape,
        in_specs=in_specs,
        out_specs=out_specs,
        scratch_shapes=list(scratch),
        compiler_params=pltpu.CompilerParams(vmem_limit_bytes=VMEM_BYTES),
        cost_estimate=pl.CostEstimate(flops=flops, bytes_accessed=moved, transcendentals=0),
    )


def swap(array, axis, size, offset):
    return lax.ppermute(array, axis, [(i, i ^ offset) for i in range(size)])


def per_device(traces, source_pos, receiver_pos, aperture_list, band_index, weight_tiles):
    samples, shots, receivers = traces.shape
    rows, cols = lax.axis_size("row"), lax.axis_size("col")
    panel = band_index.shape[0]
    steps = samples // cols
    kinds, _, depth = weight_tiles.shape
    spread_len = panel * rows // 4
    groups = rows // NF

    plane_pair = pltpu.VMEM((2, shots, receivers), BF16)
    held, own, *sends = call(
        spectra_kernel,
        [pltpu.VMEM(traces.shape, BF16)] + [plane_pair] * NF,
        [ANYWHERE],
        [WHOLE] * (1 + NF),
        [pltpu.VMEM((NF, 2, shots, receivers), BF16), pltpu.SemaphoreType.DMA((4,))],
    )(traces)
    gots = [swap(s, "row", rows, d + 1) for d, s in enumerate(sends)]
    block_shape = (2, NF, shots, receivers)
    block = call(
        rows_kernel, pltpu.VMEM(block_shape, BF16), [WHOLE] * NF, WHOLE
    )(*in_vmem(own, *gots))

    rights = [block] + [swap(block, "row", rows, d * NF) for d in range(1, groups)]
    aperture, shot_weight, stacked, tiles_turned, chosen = call(
        functools.partial(tables_kernel, float(spread_len)),
        [
            pltpu.VMEM((receivers, panel), BF16),
            pltpu.VMEM((shots, panel), F32),
            pltpu.VMEM((cols, steps, panel), F32),
            pltpu.VMEM((depth, kinds * steps), BF16),
            pltpu.VMEM((kinds, panel), F32),
        ],
        [WHOLE, ANYWHERE] + [WHOLE] * 5,
        [WHOLE] * 5,
        flops=2 * samples * shots * receivers * panel,
        moved=8 << 20,
    )(
        *in_vmem(held),
        block,
        receiver_pos.reshape(cols, receivers),
        aperture_list,
        source_pos.reshape(1, shots),
        band_index.reshape(1, panel),
        weight_tiles.reshape(kinds * steps, depth),
    )

    lefts, offsets, bit = [block], [0], cols // 2
    while bit:
        lefts += [swap(a, "col", cols, bit) for a in lefts]
        offsets += [o ^ bit for o in offsets]
        bit //= 2
    part = pltpu.VMEM((shots, 2 * receivers), BF16)
    own, *sends = call(
        functools.partial(product_kernel, tuple(offsets), groups),
        [part] * NF,
        [WHOLE] * (cols + groups),
        [WHOLE] * NF,
        [
            pltpu.VMEM((cols,) + block_shape, BF16),
            pltpu.VMEM((groups,) + block_shape, BF16),
            pltpu.VMEM((NF, shots, 2 * receivers), BF16),
        ],
    )(*in_vmem(*lefts, *rights))
    parts = in_vmem(own, *[swap(s, "row", rows, d + 1) for d, s in enumerate(sends)])

    half = cols // 2
    piece = pltpu.VMEM((half, steps, panel), F32)
    gathered = pltpu.VMEM((NF, shots, 2 * receivers), BF16)
    keep, send = call(
        stack_kernel,
        [piece, piece],
        [WHOLE] * (NF + 3),
        [WHOLE] * 2,
        [gathered, pltpu.VMEM((cols, steps, panel), F32)],
    )(*parts, *in_vmem(aperture, shot_weight, stacked))
    got = swap(send, "col", cols, half)
    primaries = call(
        primaries_kernel,
        jax.ShapeDtypeStruct(traces.shape, BF16),
        [WHOLE] * (NF + 1),
        WHOLE,
        [gathered],
        flops=1 << 20,
        moved=3 << 20,
    )(*parts, *in_vmem(held))
    while half > 1:
        half //= 2
        piece = pltpu.VMEM((half, steps, panel), F32)
        keep, send = call(halve_kernel, [piece, piece], [WHOLE] * 2, [WHOLE] * 2)(
            *in_vmem(keep, got)
        )
        got = swap(send, "col", cols, half)
    image = call(
        functools.partial(image_kernel, shots),
        jax.ShapeDtypeStruct((depth, panel), F32),
        [WHOLE] * 4 + [ANYWHERE],
        WHOLE,
    )(*in_vmem(keep, got, tiles_turned, chosen), primaries)
    return primaries, image


def solution(mesh):
    placed = (P(None, "row", "col"), P("row"), P(), P("row", None), P("row"), P())
    return jax.shard_map(
        per_device,
        mesh=mesh,
        in_specs=placed,
        out_specs=(P(None, "row", "col"), P("col", "row")),
        check_vma=False,
    )
```

```python
import functools
import math

import jax
import jax.numpy as jnp
import ml_dtypes
import numpy as np
from jax import lax
from jax.experimental import pallas as pl
from jax.experimental.pallas import tpu as pltpu
from jax.sharding import PartitionSpec as P

NFFT = 4096
NF = 4
STEP = NFFT // (4 * NF)
HALF_TURN = NFFT // (2 * STEP)
F32 = jnp.float32
BF16 = jnp.bfloat16
VMEM_BYTES = 48 * 1024 * 1024


def angle(freq, sample):
    return 2.0 * math.pi * (((2 * freq + 1) * STEP * sample) % NFFT) / NFFT


def forward_weight(freq, part, sample, samples):
    value = (math.cos, lambda a: -math.sin(a))[part](angle(freq, sample)) / math.sqrt(samples)
    return float(np.float32(value).astype(ml_dtypes.bfloat16)) if abs(value) > 1e-6 else 0.0


def weighted_sum(weights, arrays):
    total = None
    for weight, array in zip(weights, arrays):
        if abs(weight) > 1e-6:
            total = weight * array if total is None else total + weight * array
    return total


def dot(left, right):
    return jnp.dot(left, right, preferred_element_type=F32)


def wave_weights(sample):
    weights = []
    for freq in range(NF):
        weights += [math.cos(angle(freq, sample)), -math.sin(angle(freq, sample))]
    return [w / math.sqrt(NF) for w in weights]


def spectra_kernel(
    traces, aperture_list, source_pos, held, planes, mine, theirs, lists, halves, listing, places, arrived
):
    samples, shots, receivers = held.shape
    rows = shots // 4
    copies = []
    for part in range(4):
        piece = (slice(None), pl.ds(part * rows, rows))
        copies.append(pltpu.make_async_copy(traces.at[piece], held.at[piece], arrived.at[part]))
        copies[-1].start()
    for index, (given, near) in enumerate(((aperture_list, listing), (source_pos, places))):
        copies.append(pltpu.make_async_copy(given, near, arrived.at[4 + index]))
        copies[-1].start()
    lane = lax.broadcasted_iota(jnp.int32, (rows, receivers), 1)
    low = lane < receivers // 2
    for part in range(4):
        copies[part].wait()
        here = slice(part * rows, (part + 1) * rows)
        folded = []
        for sample in range(HALF_TURN):
            total = held[sample, here].astype(F32)
            for turn in range(1, samples // HALF_TURN):
                term = held[sample + turn * HALF_TURN, here].astype(F32)
                total = total - term if turn % 2 else total + term
            folded.append(total)
        for freq in range(NF):
            pair = []
            for piece in range(2):
                weights = [forward_weight(freq, piece, t, samples) for t in range(HALF_TURN)]
                pair.append(weighted_sum(weights, folded))
                planes[freq, piece, here] = pair[piece].astype(BF16)
            real, imag = pair
            turned = [pltpu.roll(p, receivers // 2, 1) for p in pair]
            halves[0, freq, here] = jnp.where(low, real, turned[1]).astype(BF16)
            halves[1, freq, here] = jnp.where(low, turned[0], imag).astype(BF16)
    copies[4].wait()
    copies[5].wait()
    tiles = listing.shape[0]
    lists[0:tiles] = listing[...]
    lists[tiles : tiles + 1, 0:shots] = places[...]
    side = lax.rem(lax.axis_index("row"), 2)
    mine[...] = halves[side]
    theirs[...] = halves[1 - side]


def pair_kernel(mine, got, both):
    both[0] = mine[...]
    both[1] = got[...]


def panel_stack(parts, aperture, shot_weight):
    lines = []
    receivers = aperture.shape[0]
    for freq in range(NF):
        for piece in range(2):
            part = parts[freq, :, piece * receivers : (piece + 1) * receivers]
            line = dot(part, aperture[...]) * shot_weight[...]
            lines.append(jnp.sum(line, axis=0, keepdims=True))
    waves = [weighted_sum(wave_weights(sample), lines) for sample in range(HALF_TURN)]
    return jnp.concatenate(waves, axis=0)


def product_kernel(levels, left, *refs):
    rights = refs[:levels]
    apertures, shot_weights, mine, theirs, waves, right = refs[levels:]
    level = lax.axis_index("row") // 2
    for offset, got in enumerate(rights):
        right[level ^ offset] = got[...]
    _, _, _, shots, lanes = left.shape
    scale = -1.0 / math.sqrt(2 * levels * shots)
    step = min(2, levels)
    for freq in range(NF):
        total = None
        for first in range(0, levels, step):
            inner = range(first, first + step)
            near = jnp.concatenate(
                [left[k, :, freq].reshape(2 * shots, lanes) for k in inner], axis=1
            )
            far = []
            for k in inner:
                real, imag = right[k, freq, 0], right[k, freq, 1]
                far.append(jnp.concatenate([real, imag], axis=1))
                far.append(jnp.concatenate([-imag, real], axis=1))
            term = dot(near, jnp.concatenate(far, axis=0))
            total = term if total is None else total + term
        total = total * scale
        mine[freq] = total[:shots].astype(BF16)
        theirs[freq] = total[shots:].astype(BF16)
    waves[...] = panel_stack(theirs, apertures.at[1], shot_weights.at[1])


def tables_kernel(
    spread_len, left, got_lists, receiver_pos, aperture_list, source_pos, apertures, shot_weights
):
    del left
    _, receivers, panel = apertures.shape
    shots = shot_weights.shape[1]
    tiles, listed = aperture_list.shape
    width = panel // tiles
    row, col = lax.axis_index("row"), lax.axis_index("col")

    def upright(line, length):
        at_row = lax.broadcasted_iota(jnp.int32, (length, length), 0)
        at_lane = lax.broadcasted_iota(jnp.int32, (length, length), 1)
        return jnp.sum(jnp.where(at_row == at_lane, line.astype(F32), 0.0), axis=1, keepdims=True)

    def taper(positions, length, first):
        columns = (lax.broadcasted_iota(jnp.int32, (length, panel), 1) + first).astype(F32)
        offset = (positions - columns) / spread_len
        return 1.0 / (1.0 + offset * offset)

    position = upright(receiver_pos[pl.ds(col, 1)], receivers)
    receiver = lax.broadcasted_iota(jnp.int32, (receivers, listed), 0) + col * receivers
    ones = jnp.ones((listed, width), BF16)
    sources = (source_pos[...], got_lists[tiles : tiles + 1, 0:shots])
    for index, lists in enumerate((aperture_list, got_lists)):
        first = (row ^ index) * panel
        near = taper(position, receivers, first)
        for tile in range(tiles):
            hits = jnp.where(lists[tile : tile + 1] == receiver, 1.0, 0.0).astype(BF16)
            counts = dot(hits, ones)
            here = slice(tile * width, (tile + 1) * width)
            weighted = counts * near[:, here] * (2.0 / math.sqrt(listed))
            apertures[index, :, here] = weighted.astype(BF16)
        shot_weights[index] = taper(upright(sources[index], shots), shots, first)


def subtract_waves(band, columns, waves):
    steps = columns.shape[0]
    start = band * steps
    sign = -1.0 if (start // HALF_TURN) % 2 else 1.0
    first = start % HALF_TURN
    return columns - sign * waves[first : first + steps]


def own_stack_kernel(
    mine, held, apertures, shot_weights, band_index, weight_tiles, columns, tiles_turned, chosen
):
    waves = panel_stack(mine, apertures.at[0], shot_weights.at[0])
    bands, steps, _ = columns.shape
    for band in range(bands):
        lines = []
        for step in range(steps):
            line = dot(held[band * steps + step], apertures[0])
            lines.append(jnp.sum(line * shot_weights[0], axis=0, keepdims=True))
        columns[band] = subtract_waves(band, jnp.concatenate(lines, axis=0), waves)
    tiles_turned[...] = weight_tiles[...].astype(F32).T.astype(BF16)
    kind = lax.broadcasted_iota(jnp.int32, chosen.shape, 0)
    chosen[...] = jnp.where(band_index[...] == kind, 1.0, 0.0)


def column_kernel(columns, got, *refs):
    total = refs[-1]
    col = lax.axis_index("col")
    waves = got[...]
    for band in range(columns.shape[0]):
        total[band] = subtract_waves(band, columns[band], waves)
    for offset, out in enumerate(refs[:-1]):
        out[...] = total[col ^ offset]


def primaries_kernel(mine, got, held, out, token):
    samples, shots, receivers = held.shape
    rows = 16
    for start in range(0, shots, rows):
        here = slice(start, start + rows)
        parts = []
        for freq in range(NF):
            both = mine[freq, here].astype(F32) + got[freq, here].astype(F32)
            parts += [both[:, :receivers], both[:, receivers:]]
        for sample in range(HALF_TURN):
            wave = weighted_sum(wave_weights(sample), parts)
            for turn in range(samples // HALF_TURN):
                at = sample + turn * HALF_TURN
                trace = held[at, here].astype(F32)
                out[at, here] = (trace + wave if turn % 2 else trace - wave).astype(BF16)
    token[...] = jnp.zeros_like(token)


def image_kernel(shots, bands, *refs):
    parts = refs[:bands]
    tiles_turned, chosen, _, image = refs[bands:]
    total = parts[0][...]
    for part in parts[1:]:
        total = total + part[...]
    column_stack = total / math.sqrt(shots)
    steps, panel = column_stack.shape
    kinds = chosen.shape[0]
    rounded = column_stack.astype(BF16).astype(F32)
    widened = jnp.where(chosen[...][:, None, :] > 0.5, rounded[None], 0.0)
    image[...] = dot(tiles_turned[...], widened.reshape(kinds * steps, panel).astype(BF16))


WHOLE = pl.BlockSpec(memory_space=pltpu.VMEM)
IN_HBM = pl.BlockSpec(memory_space=pltpu.HBM)


def in_vmem(*arrays):
    return [pltpu.with_memory_space_constraint(a, pltpu.VMEM) for a in arrays]


def call(body, out_shape, in_specs, out_specs, scratch=(), flops=0, moved=0):
    return pl.pallas_call(
        body,
        out_shape=out_shape,
        in_specs=in_specs,
        out_specs=out_specs,
        scratch_shapes=list(scratch),
        compiler_params=pltpu.CompilerParams(vmem_limit_bytes=VMEM_BYTES),
        cost_estimate=pl.CostEstimate(flops=flops, bytes_accessed=moved, transcendentals=0),
    )


def swap(array, axis, size, offset):
    return lax.ppermute(array, axis, [(i, i ^ offset) for i in range(size)])


def per_device(traces, source_pos, receiver_pos, aperture_list, band_index, weight_tiles):
    samples, shots, receivers = traces.shape
    rows, cols = lax.axis_size("row"), lax.axis_size("col")
    panel = band_index.shape[0]
    steps = samples // cols
    kinds, _, depth = weight_tiles.shape
    spread_len = panel * rows // 4
    levels = rows // 2
    tiles, listed = aperture_list.shape
    assert receivers == 2 * shots and levels == cols

    plane_shape = (NF, 2, shots, receivers)
    half_shape = (NF, shots, receivers)
    part = pltpu.VMEM((NF, shots, 2 * receivers), BF16)
    positions = source_pos.reshape(1, shots)
    held, planes, mine, theirs, lists = call(
        spectra_kernel,
        [
            pltpu.VMEM(traces.shape, BF16),
            pltpu.VMEM(plane_shape, BF16),
            pltpu.VMEM(half_shape, BF16),
            pltpu.VMEM(half_shape, BF16),
            pltpu.VMEM((2 * tiles, listed), jnp.int32),
        ],
        [IN_HBM] * 3,
        [WHOLE] * 5,
        [
            pltpu.VMEM((2,) + half_shape, BF16),
            pltpu.VMEM(aperture_list.shape, jnp.int32),
            pltpu.VMEM(positions.shape, jnp.int32),
            pltpu.SemaphoreType.DMA((6,)),
        ],
    )(*[pltpu.with_memory_space_constraint(a, pltpu.HBM) for a in (traces, aperture_list, positions)])
    rights = [planes] + [swap(planes, "row", rows, 2 * d) for d in range(1, levels)]
    both = call(pair_kernel, pltpu.VMEM((2,) + half_shape, BF16), [WHOLE] * 2, WHOLE)(
        *in_vmem(mine, swap(theirs, "row", rows, 1))
    )
    left = lax.all_gather(both, "col")
    apertures, shot_weights = call(
        functools.partial(tables_kernel, float(spread_len)),
        [pltpu.VMEM((2, receivers, panel), BF16), pltpu.VMEM((2, shots, panel), F32)],
        [WHOLE] * 5,
        [WHOLE] * 2,
        moved=2 << 20,
    )(
        *in_vmem(left, swap(lists, "row", rows, 1)),
        receiver_pos.reshape(cols, receivers),
        aperture_list,
        positions,
    )
    mine, theirs, waves = call(
        functools.partial(product_kernel, levels),
        [part, part, pltpu.VMEM((HALF_TURN, panel), F32)],
        [WHOLE] * (levels + 3),
        [WHOLE] * 3,
        [pltpu.VMEM((levels,) + plane_shape, BF16)],
    )(*in_vmem(left, *rights, apertures, shot_weights))
    got_waves = swap(waves, "row", rows, 1)
    got_part = swap(theirs, "row", rows, 1)
    columns, tiles_turned, chosen = call(
        own_stack_kernel,
        [
            pltpu.VMEM((cols, steps, panel), F32),
            pltpu.VMEM((depth, kinds * steps), BF16),
            pltpu.VMEM((kinds, panel), F32),
        ],
        [WHOLE] * 6,
        [WHOLE] * 3,
        flops=2 * samples * shots * receivers * panel,
        moved=1 << 20,
    )(
        *in_vmem(mine, held, apertures, shot_weights),
        band_index.reshape(1, panel),
        weight_tiles.reshape(kinds * steps, depth),
    )
    band = pltpu.VMEM((steps, panel), F32)
    own, *sends = call(
        column_kernel,
        [band] * cols,
        [WHOLE] * 2,
        [WHOLE] * cols,
        [pltpu.VMEM((cols, steps, panel), F32)],
    )(*in_vmem(columns, got_waves))
    bands = [own] + [swap(s, "col", cols, d + 1) for d, s in enumerate(sends)]
    primaries, token = call(
        primaries_kernel,
        [jax.ShapeDtypeStruct(traces.shape, BF16), pltpu.VMEM((8, 128), F32)],
        [WHOLE] * 3,
        [WHOLE] * 2,
        flops=1 << 20,
        moved=3 << 20,
    )(*in_vmem(mine, got_part, held))
    image = call(
        functools.partial(image_kernel, shots, cols),
        jax.ShapeDtypeStruct((depth, panel), F32),
        [WHOLE] * (cols + 3),
        WHOLE,
    )(*in_vmem(*bands, tiles_turned, chosen, token))
    return primaries, image


def solution(mesh):
    placed = (P(None, "row", "col"), P("row"), P(), P("row", None), P("row"), P())
    return jax.shard_map(
        per_device,
        mesh=mesh,
        in_specs=placed,
        out_specs=(P(None, "row", "col"), P("col", "row")),
        check_vma=False,
    )
```

```python
import functools
import math

import jax
import jax.numpy as jnp
import ml_dtypes
import numpy as np
from jax import lax
from jax.experimental import pallas as pl
from jax.experimental.pallas import tpu as pltpu
from jax.sharding import PartitionSpec as P

NFFT = 4096
NF = 4
STEP = NFFT // (4 * NF)
HALF_TURN = NFFT // (2 * STEP)
F32 = jnp.float32
BF16 = jnp.bfloat16
PARTS = 2


def routes(levels):
    if levels == 4:
        return [[2, 3, 1, 0], [1, 0, 3, 2], [3, 2, 0, 1]]
    return [[(a + d) % levels for a in range(levels)] for d in range(1, levels)]


LINKT = BF16
VMEM_BYTES = 48 * 1024 * 1024


def angle(freq, sample):
    return 2.0 * math.pi * (((2 * freq + 1) * STEP * sample) % NFFT) / NFFT


def forward_weight(freq, part, sample, samples):
    value = (math.cos, lambda a: -math.sin(a))[part](angle(freq, sample)) / math.sqrt(samples)
    return float(np.float32(value).astype(ml_dtypes.bfloat16)) if abs(value) > 1e-6 else 0.0


def weighted_sum(weights, arrays):
    total = None
    for weight, array in zip(weights, arrays):
        if abs(weight) > 1e-6:
            total = weight * array if total is None else total + weight * array
    return total


def dot(left, right):
    return jnp.dot(left, right, preferred_element_type=F32)


def wave_weights(sample):
    weights = []
    for freq in range(NF):
        weights += [math.cos(angle(freq, sample)), -math.sin(angle(freq, sample))]
    return [w / math.sqrt(NF) for w in weights]


DIGIT = 128


def digit_rows(tiles, listed):
    used = 2 * tiles * (listed // DIGIT) + 2
    return -(-used // 16) * 16


def spectra_kernel(
    traces, aperture_list, source_pos, receiver_pos, band_index, weight_tiles,
    held, planes, mine, theirs, lists, places, stations, kinds, tiles_near,
    halves, digits, arrived,
):
    samples, shots, receivers = held.shape
    rows = shots // PARTS
    copies = []
    for part in range(PARTS):
        piece = (slice(None), pl.ds(part * rows, rows))
        copies.append(pltpu.make_async_copy(traces.at[piece], held.at[piece], arrived.at[part]))
        copies[-1].start()
    given = (aperture_list, source_pos, receiver_pos, band_index, weight_tiles)
    for index, near in enumerate((lists, places, stations, kinds, tiles_near)):
        copies.append(pltpu.make_async_copy(given[index], near, arrived.at[PARTS + index]))
        copies[-1].start()
    lane = lax.broadcasted_iota(jnp.int32, (rows, receivers), 1)
    low = lane < receivers // 2
    for part in range(PARTS):
        copies[part].wait()
        here = slice(part * rows, (part + 1) * rows)
        folded = []
        for sample in range(HALF_TURN):
            total = held[sample, here].astype(F32)
            for turn in range(1, samples // HALF_TURN):
                term = held[sample + turn * HALF_TURN, here].astype(F32)
                total = total - term if turn % 2 else total + term
            folded.append(total)
        for freq in range(NF):
            pair = []
            for piece in range(2):
                weights = [forward_weight(freq, piece, t, samples) for t in range(HALF_TURN)]
                pair.append(weighted_sum(weights, folded))
                planes[freq, piece, here] = pair[piece].astype(BF16)
            real, imag = pair
            turned = [pltpu.roll(p, receivers // 2, 1) for p in pair]
            halves[0, freq, here] = jnp.where(low, real, turned[1]).astype(BF16)
            halves[1, freq, here] = jnp.where(low, turned[0], imag).astype(BF16)
    for copy in copies[PARTS:]:
        copy.wait()
    tiles, listed = lists.shape
    groups = listed // DIGIT
    digits[...] = jnp.zeros_like(digits)
    for group in range(groups):
        some = lists[:, group * DIGIT : (group + 1) * DIGIT]
        start = 2 * group * tiles
        digits[start : start + tiles] = (some >> 7).astype(F32)
        digits[start + tiles : start + 2 * tiles] = (some & (DIGIT - 1)).astype(F32)
    start = 2 * groups * tiles
    digits[start : start + 1, 0:shots] = (places[...] >> 7).astype(F32)
    digits[start + 1 : start + 2, 0:shots] = (places[...] & (DIGIT - 1)).astype(F32)
    side = lax.rem(lax.axis_index("row"), 2)
    mine[...] = halves[side]
    theirs[0 : NF * shots] = halves[1 - side].reshape(NF * shots, receivers)
    theirs[NF * shots :] = digits[...].astype(BF16)


def pair_kernel(mine, got, both):
    both[0] = mine[...]
    both[1] = got[0 : mine.shape[0] * mine.shape[1]].reshape(mine.shape)


def panel_stack(parts, aperture, shot_weight):
    lines = []
    receivers = aperture.shape[0]
    for freq in range(NF):
        for piece in range(2):
            part = parts[freq, :, piece * receivers : (piece + 1) * receivers]
            line = dot(part, aperture[...]) * shot_weight[...]
            lines.append(jnp.sum(line, axis=0, keepdims=True))
    waves = [weighted_sum(wave_weights(sample), lines) for sample in range(HALF_TURN)]
    return jnp.concatenate(waves, axis=0)


def product_kernel(levels, left, *refs):
    rights = refs[:levels]
    apertures, shot_weights, mine, theirs, waves, right = refs[levels:]
    level = lax.axis_index("row") // 2
    right[level] = rights[0][...]
    for to, got in zip(routes(levels), rights[1:]):
        origin = sum(jnp.where(level == there, here, 0) for here, there in enumerate(to))
        right[origin] = got[...]
    _, _, _, shots, lanes = left.shape
    scale = -1.0 / math.sqrt(2 * levels * shots)
    step = min(2, levels)
    for freq in range(NF):
        total = None
        for first in range(0, levels, step):
            inner = range(first, first + step)
            near = jnp.concatenate(
                [left[k, :, freq].reshape(2 * shots, lanes) for k in inner], axis=1
            )
            far = []
            for k in inner:
                real, imag = right[k, freq, 0], right[k, freq, 1]
                far.append(jnp.concatenate([real, imag], axis=1))
                far.append(jnp.concatenate([-imag, real], axis=1))
            term = dot(near, jnp.concatenate(far, axis=0))
            total = term if total is None else total + term
        total = total * scale
        mine[freq] = total[:shots].astype(BF16)
        theirs[freq] = total[shots:].astype(BF16)
    waves[...] = panel_stack(theirs, apertures.at[1], shot_weights.at[1]).astype(waves.dtype)


def tables_kernel(
    spread_len, left, got, stations, lists, places, apertures, shot_weights, digits
):
    del left
    _, receivers, panel = apertures.shape
    shots = shot_weights.shape[1]
    tiles, listed = lists.shape
    groups = listed // DIGIT
    width = panel // tiles
    row, col = lax.axis_index("row"), lax.axis_index("col")

    def upright(line, length):
        at_row = lax.broadcasted_iota(jnp.int32, (length, length), 0)
        at_lane = lax.broadcasted_iota(jnp.int32, (length, length), 1)
        return jnp.sum(jnp.where(at_row == at_lane, line.astype(F32), 0.0), axis=1, keepdims=True)

    def taper(positions, length, first):
        columns = (lax.broadcasted_iota(jnp.int32, (length, panel), 1) + first).astype(F32)
        offset = (positions - columns) / spread_len
        return 1.0 / (1.0 + offset * offset)

    position = upright(stations[pl.ds(col, 1)], receivers)
    receiver = lax.broadcasted_iota(jnp.int32, (receivers, listed), 0) + col * receivers
    receiver = receiver.astype(F32)
    ones = jnp.ones((listed, width), BF16)
    digits[...] = got[NF * shots :].astype(F32)
    theirs = []
    for group in range(groups):
        start = 2 * group * tiles
        high, low = digits[start : start + tiles], digits[start + tiles : start + 2 * tiles]
        theirs.append(high * DIGIT + low)
    start = 2 * groups * tiles
    there = digits[start : start + 1, 0:shots] * DIGIT + digits[start + 1 : start + 2, 0:shots]
    sources = (places[...].astype(F32), there)
    for index, listing in enumerate((lists[...].astype(F32), jnp.concatenate(theirs, axis=1))):
        first = (row ^ index) * panel
        near = taper(position, receivers, first)
        for tile in range(tiles):
            hits = jnp.where(listing[tile : tile + 1] == receiver, 1.0, 0.0).astype(BF16)
            counts = dot(hits, ones)
            here = slice(tile * width, (tile + 1) * width)
            weighted = counts * near[:, here] * (2.0 / math.sqrt(listed))
            apertures[index, :, here] = weighted.astype(BF16)
        shot_weights[index] = taper(upright(sources[index], shots), shots, first)


def subtract_waves(band, columns, waves):
    steps = columns.shape[0]
    start = band * steps
    sign = -1.0 if (start // HALF_TURN) % 2 else 1.0
    first = start % HALF_TURN
    return columns - sign * waves[first : first + steps]


def own_stack_kernel(
    mine, held, apertures, shot_weights, kinds, tiles_near, columns, tiles_turned, chosen
):
    waves = panel_stack(mine, apertures.at[0], shot_weights.at[0])
    bands, steps, _ = columns.shape
    for band in range(bands):
        lines = []
        for step in range(steps):
            line = dot(held[band * steps + step], apertures[0])
            lines.append(jnp.sum(line * shot_weights[0], axis=0, keepdims=True))
        columns[band] = subtract_waves(band, jnp.concatenate(lines, axis=0), waves)
    tiles_turned[...] = tiles_near[...].astype(F32).T.astype(BF16)
    kind = lax.broadcasted_iota(jnp.int32, chosen.shape, 0)
    chosen[...] = jnp.where(kinds[...] == kind, 1.0, 0.0)


def column_kernel(columns, got, *refs):
    total = refs[-1]
    col = lax.axis_index("col")
    waves = got[...].astype(F32)
    for band in range(columns.shape[0]):
        total[band] = subtract_waves(band, columns[band], waves)
    for offset, out in enumerate(refs[:-1]):
        out[...] = total[col ^ offset].astype(out.dtype)


def primaries_kernel(mine, got, held, out, token):
    samples, shots, receivers = held.shape
    rows = 16
    for start in range(0, shots, rows):
        here = slice(start, start + rows)
        parts = []
        for freq in range(NF):
            both = mine[freq, here].astype(F32) + got[freq, here].astype(F32)
            parts += [both[:, :receivers], both[:, receivers:]]
        for sample in range(HALF_TURN):
            wave = weighted_sum(wave_weights(sample), parts)
            for turn in range(samples // HALF_TURN):
                at = sample + turn * HALF_TURN
                trace = held[at, here].astype(F32)
                out[at, here] = (trace + wave if turn % 2 else trace - wave).astype(BF16)
    token[...] = jnp.zeros_like(token)


def image_kernel(shots, bands, *refs):
    parts = refs[:bands]
    tiles_turned, chosen, _, image = refs[bands:]
    total = parts[0][...]
    for part in parts[1:]:
        total = total + part[...].astype(F32)
    column_stack = total / math.sqrt(shots)
    steps, panel = column_stack.shape
    kinds = chosen.shape[0]
    rounded = column_stack.astype(BF16).astype(F32)
    widened = jnp.where(chosen[...][:, None, :] > 0.5, rounded[None], 0.0)
    image[...] = dot(tiles_turned[...], widened.reshape(kinds * steps, panel).astype(BF16))


WHOLE = pl.BlockSpec(memory_space=pltpu.VMEM)
IN_HBM = pl.BlockSpec(memory_space=pltpu.HBM)


def in_vmem(*arrays):
    return [pltpu.with_memory_space_constraint(a, pltpu.VMEM) for a in arrays]


def in_hbm(*arrays):
    return [pltpu.with_memory_space_constraint(a, pltpu.HBM) for a in arrays]


def call(body, out_shape, in_specs, out_specs, scratch=(), flops=0, moved=0):
    return pl.pallas_call(
        body,
        out_shape=out_shape,
        in_specs=in_specs,
        out_specs=out_specs,
        scratch_shapes=list(scratch),
        compiler_params=pltpu.CompilerParams(vmem_limit_bytes=VMEM_BYTES),
        cost_estimate=pl.CostEstimate(flops=flops, bytes_accessed=moved, transcendentals=0),
    )


def swap(array, axis, size, offset):
    return lax.ppermute(array, axis, [(i, i ^ offset) for i in range(size)])


def per_device(traces, source_pos, receiver_pos, aperture_list, band_index, weight_tiles):
    samples, shots, receivers = traces.shape
    rows, cols = lax.axis_size("row"), lax.axis_size("col")
    panel = band_index.shape[0]
    steps = samples // cols
    kinds, _, depth = weight_tiles.shape
    spread_len = panel * rows // 4
    levels = rows // 2
    tiles, listed = aperture_list.shape
    assert receivers == 2 * shots and levels == cols

    plane_shape = (NF, 2, shots, receivers)
    half_shape = (NF, shots, receivers)
    part = pltpu.VMEM((NF, shots, 2 * receivers), BF16)
    extra = digit_rows(tiles, listed)
    held, planes, mine, theirs, lists, places, stations, near_kinds, tiles_near = call(
        spectra_kernel,
        [
            pltpu.VMEM(traces.shape, BF16),
            pltpu.VMEM(plane_shape, BF16),
            pltpu.VMEM(half_shape, BF16),
            pltpu.VMEM((NF * shots + extra, receivers), BF16),
            pltpu.VMEM(aperture_list.shape, jnp.int32),
            pltpu.VMEM((1, shots), jnp.int32),
            pltpu.VMEM((cols, receivers), jnp.int32),
            pltpu.VMEM((1, panel), jnp.int32),
            pltpu.VMEM((kinds * steps, depth), BF16),
        ],
        [IN_HBM] * 6,
        [WHOLE] * 9,
        [
            pltpu.VMEM((2,) + half_shape, BF16),
            pltpu.VMEM((extra, DIGIT), F32),
            pltpu.SemaphoreType.DMA((PARTS + 5,)),
        ],
    )(
        *in_hbm(
            traces,
            aperture_list,
            source_pos.reshape(1, shots),
            receiver_pos.reshape(cols, receivers),
            band_index.reshape(1, panel),
            weight_tiles.reshape(kinds * steps, depth),
        )
    )
    rights = [planes] + [
        lax.ppermute(planes, "row", [(2 * a + x, 2 * b + x) for a, b in enumerate(to) for x in range(2)])
        for to in routes(levels)
    ]
    got = swap(theirs, "row", rows, 1)
    both = call(pair_kernel, pltpu.VMEM((2,) + half_shape, BF16), [WHOLE] * 2, WHOLE)(
        *in_vmem(mine, got)
    )
    left = lax.all_gather(both, "col")
    apertures, shot_weights = call(
        functools.partial(tables_kernel, float(spread_len)),
        [pltpu.VMEM((2, receivers, panel), BF16), pltpu.VMEM((2, shots, panel), F32)],
        [WHOLE] * 5,
        [WHOLE] * 2,
        [pltpu.VMEM((extra, DIGIT), F32)],
    )(*in_vmem(left, got, stations, lists, places))
    mine, theirs, waves = call(
        functools.partial(product_kernel, levels),
        [part, part, pltpu.VMEM((HALF_TURN, panel), LINKT)],
        [WHOLE] * (levels + 3),
        [WHOLE] * 3,
        [pltpu.VMEM((levels,) + plane_shape, BF16)],
    )(*in_vmem(left, *rights, apertures, shot_weights))
    got_waves = swap(waves, "row", rows, 1)
    got_part = swap(theirs, "row", rows, 1)
    columns, tiles_turned, chosen = call(
        own_stack_kernel,
        [
            pltpu.VMEM((cols, steps, panel), F32),
            pltpu.VMEM((depth, kinds * steps), BF16),
            pltpu.VMEM((kinds, panel), F32),
        ],
        [WHOLE] * 6,
        [WHOLE] * 3,
        flops=1 << 34,
    )(*in_vmem(mine, held, apertures, shot_weights, near_kinds, tiles_near))
    band = pltpu.VMEM((steps, panel), F32)
    own, *sends = call(
        column_kernel,
        [band] + [pltpu.VMEM((steps, panel), LINKT)] * (cols - 1),
        [WHOLE] * 2,
        [WHOLE] * cols,
        [pltpu.VMEM((cols, steps, panel), F32)],
        flops=1 << 34,
    )(*in_vmem(columns, got_waves))
    bands = [own] + [swap(s, "col", cols, d + 1) for d, s in enumerate(sends)]
    primaries, token = call(
        primaries_kernel,
        [jax.ShapeDtypeStruct(traces.shape, BF16), pltpu.VMEM((8, 128), F32)],
        [WHOLE] * 3,
        [WHOLE] * 2,
        flops=1 << 20,
        moved=3 << 20,
    )(*in_vmem(mine, got_part, held))
    image = call(
        functools.partial(image_kernel, shots, cols),
        jax.ShapeDtypeStruct((depth, panel), F32),
        [WHOLE] * (cols + 3),
        WHOLE,
    )(*in_vmem(*bands, tiles_turned, chosen, token))
    return primaries, image


def solution(mesh):
    placed = (P(None, "row", "col"), P("row"), P(), P("row", None), P("row"), P())
    return jax.shard_map(
        per_device,
        mesh=mesh,
        in_specs=placed,
        out_specs=(P(None, "row", "col"), P("col", "row")),
        check_vma=False,
    )
```

```python
import functools
import math

import jax
import jax.numpy as jnp
import ml_dtypes
import numpy as np
from jax import lax
from jax.experimental import pallas as pl
from jax.experimental.pallas import tpu as pltpu
from jax.sharding import PartitionSpec as P

NFFT = 4096
NF = 4
STEP = NFFT // (4 * NF)
HALF_TURN = NFFT // (2 * STEP)
F32 = jnp.float32
BF16 = jnp.bfloat16
PARTS = 2


def routes(levels):
    if levels == 4:
        return [[2, 3, 1, 0], [1, 0, 3, 2], [3, 2, 0, 1]]
    return [[(a + d) % levels for a in range(levels)] for d in range(1, levels)]


LINKT = BF16
VMEM_BYTES = 48 * 1024 * 1024


def angle(freq, sample):
    return 2.0 * math.pi * (((2 * freq + 1) * STEP * sample) % NFFT) / NFFT


def forward_weight(freq, part, sample, samples):
    value = (math.cos, lambda a: -math.sin(a))[part](angle(freq, sample)) / math.sqrt(samples)
    return float(np.float32(value).astype(ml_dtypes.bfloat16)) if abs(value) > 1e-6 else 0.0


def weighted_sum(weights, arrays):
    total = None
    for weight, array in zip(weights, arrays):
        if abs(weight) > 1e-6:
            total = weight * array if total is None else total + weight * array
    return total


def dot(left, right):
    return jnp.dot(left, right, preferred_element_type=F32)


def wave_weights(sample):
    weights = []
    for freq in range(NF):
        weights += [math.cos(angle(freq, sample)), -math.sin(angle(freq, sample))]
    return [w / math.sqrt(NF) for w in weights]


DIGIT = 128


def digit_rows(tiles, listed):
    used = 2 * tiles * (listed // DIGIT) + 2
    return -(-used // 16) * 16


def upright(line):
    length = line.shape[1]
    at_row = lax.broadcasted_iota(jnp.int32, (length, length), 0)
    at_lane = lax.broadcasted_iota(jnp.int32, (length, length), 1)
    return jnp.sum(jnp.where(at_row == at_lane, line.astype(F32), 0.0), axis=1, keepdims=True)


def taper(positions, panel, first, spread_len):
    columns = (lax.broadcasted_iota(jnp.int32, (positions.shape[0], panel), 1) + first).astype(F32)
    offset = (positions - columns) / spread_len
    return 1.0 / (1.0 + offset * offset)


def fill_aperture(aperture, listing, near):
    receivers, panel = aperture.shape
    tiles, listed = listing.shape
    width = panel // tiles
    receiver = lax.broadcasted_iota(jnp.int32, (receivers, listed), 0)
    receiver = (receiver + lax.axis_index("col") * receivers).astype(F32)
    ones = jnp.ones((listed, width), BF16)
    for tile in range(tiles):
        hits = jnp.where(listing[tile : tile + 1] == receiver, 1.0, 0.0).astype(BF16)
        here = slice(tile * width, (tile + 1) * width)
        weighted = dot(hits, ones) * near[:, here] * (2.0 / math.sqrt(listed))
        aperture[:, here] = weighted.astype(BF16)


def spectra_kernel(
    traces, aperture_list, source_pos, receiver_pos, band_index, weight_tiles,
    held, planes, mine, theirs, lists, places, stations, kinds, tiles_near,
    halves, digits, arrived,
):
    samples, shots, receivers = held.shape
    rows = shots // PARTS
    copies = []
    for part in range(PARTS):
        piece = (slice(None), pl.ds(part * rows, rows))
        copies.append(pltpu.make_async_copy(traces.at[piece], held.at[piece], arrived.at[part]))
    given = (aperture_list, source_pos, receiver_pos, band_index, weight_tiles)
    for index, near in enumerate((lists, places, stations, kinds, tiles_near)):
        copies.append(pltpu.make_async_copy(given[index], near, arrived.at[PARTS + index]))
    for copy in copies:
        copy.start()
    lane = lax.broadcasted_iota(jnp.int32, (rows, receivers), 1)
    low = lane < receivers // 2
    for part in range(PARTS):
        copies[part].wait()
        here = slice(part * rows, (part + 1) * rows)
        folded = []
        for sample in range(HALF_TURN):
            total = held[sample, here].astype(F32)
            for turn in range(1, samples // HALF_TURN):
                term = held[sample + turn * HALF_TURN, here].astype(F32)
                total = total - term if turn % 2 else total + term
            folded.append(total)
        for freq in range(NF):
            pair = []
            for piece in range(2):
                weights = [forward_weight(freq, piece, t, samples) for t in range(HALF_TURN)]
                pair.append(weighted_sum(weights, folded))
                planes[freq, piece, here] = pair[piece].astype(BF16)
            real, imag = pair
            turned = [pltpu.roll(p, receivers // 2, 1) for p in pair]
            halves[0, freq, here] = jnp.where(low, real, turned[1]).astype(BF16)
            halves[1, freq, here] = jnp.where(low, turned[0], imag).astype(BF16)
    for copy in copies[PARTS:]:
        copy.wait()
    tiles, listed = lists.shape
    groups = listed // DIGIT
    digits[...] = jnp.zeros_like(digits)
    for group in range(groups):
        some = lists[:, group * DIGIT : (group + 1) * DIGIT]
        start = 2 * group * tiles
        digits[start : start + tiles] = (some >> 7).astype(F32)
        digits[start + tiles : start + 2 * tiles] = (some & (DIGIT - 1)).astype(F32)
    start = 2 * groups * tiles
    digits[start : start + 1, 0:shots] = (places[...] >> 7).astype(F32)
    digits[start + 1 : start + 2, 0:shots] = (places[...] & (DIGIT - 1)).astype(F32)
    side = lax.rem(lax.axis_index("row"), 2)
    mine[...] = halves[side]
    theirs[0 : NF * shots] = halves[1 - side].reshape(NF * shots, receivers)
    theirs[NF * shots :] = digits[...].astype(BF16)


def pair_kernel(mine, got, both):
    both[0] = mine[...]
    both[1] = got[0 : mine.shape[0] * mine.shape[1]].reshape(mine.shape)


def shot_sums(lines, aperture, shot_weight):
    shots, panel = shot_weight.shape
    stacked = dot(lines, aperture[...]).reshape(lines.shape[0] // shots, shots, panel)
    return jnp.sum(stacked * shot_weight[...][None], axis=1)


def panel_stack(parts, aperture, shot_weight):
    receivers = aperture.shape[0]
    both = parts[...]
    lines = jnp.concatenate(
        [both[freq][:, lanes] for freq in range(NF) for lanes in (slice(0, receivers), slice(receivers, None))]
    )
    sums = shot_sums(lines, aperture, shot_weight)
    rows = [sums[k : k + 1] for k in range(2 * NF)]
    waves = [weighted_sum(wave_weights(sample), rows) for sample in range(HALF_TURN)]
    return jnp.concatenate(waves, axis=0)


def level_blocks(rights, levels):
    level = lax.axis_index("row") // 2
    blocks = [(level, rights[0])]
    for to, got in zip(routes(levels), rights[1:]):
        blocks.append((sum(jnp.where(level == there, here, 0) for here, there in enumerate(to)), got))
    return blocks


def product(part, freq, left, blocks):
    step = min(2, len(blocks))
    total = None
    for first in range(0, len(blocks), step):
        some = blocks[first : first + step]
        near = jnp.concatenate([left[origin, part, freq] for origin, _ in some], axis=1)
        far = []
        for _, right in some:
            real, imag = right[freq, 0], right[freq, 1]
            far.append(jnp.concatenate([real, imag], axis=1))
            far.append(jnp.concatenate([-imag, real], axis=1))
        term = dot(near, jnp.concatenate(far, axis=0))
        total = term if total is None else total + term
    surface = 2 * len(blocks) * left.shape[3]
    return (total * (-1.0 / math.sqrt(surface))).astype(BF16)


def product_kernel(levels, left, *refs):
    aperture, shot_weight, theirs, waves = refs[levels:]
    blocks = level_blocks(refs[:levels], levels)
    for freq in range(NF):
        theirs[freq] = product(1, freq, left, blocks)
    waves[...] = panel_stack(theirs, aperture, shot_weight).astype(waves.dtype)


def tables_kernel(
    spread_len, left, got, lists, places, stations, aperture, shot_weight, their_aperture, their_weight, digits
):
    del left
    shots, panel = shot_weight.shape
    tiles, listed = lists.shape
    row, col = lax.axis_index("row"), lax.axis_index("col")
    digits[...] = got[NF * shots :].astype(F32)
    listing = []
    start = 0
    for _ in range(listed // DIGIT):
        high, low = digits[start : start + tiles], digits[start + tiles : start + 2 * tiles]
        listing.append(high * DIGIT + low)
        start += 2 * tiles
    there = digits[start : start + 1, 0:shots] * DIGIT + digits[start + 1 : start + 2, 0:shots]
    position = upright(stations[pl.ds(col, 1)])
    for first, some, sources, table, weight in (
        (row * panel, lists[...].astype(F32), places[...], aperture, shot_weight),
        ((row ^ 1) * panel, jnp.concatenate(listing, axis=1), there, their_aperture, their_weight),
    ):
        fill_aperture(table, some, taper(position, panel, first, spread_len))
        weight[...] = taper(upright(sources), panel, first, spread_len)


def subtract_waves(band, columns, waves):
    steps = columns.shape[0]
    start = band * steps
    sign = -1.0 if (start // HALF_TURN) % 2 else 1.0
    first = start % HALF_TURN
    return columns - sign * waves[first : first + steps]


def own_stack_kernel(levels, left, *refs):
    (
        theirs, held, aperture, shot_weight, kinds, tiles_near,
        mine, columns, tiles_turned, chosen, send,
    ) = refs[levels:]
    blocks = level_blocks(refs[:levels], levels)
    for freq in range(NF):
        mine[freq] = product(0, freq, left, blocks)
    waves = panel_stack(mine, aperture, shot_weight)
    bands, steps, _ = columns.shape
    _, shots, receivers = held.shape
    for band in range(bands):
        lines = held[band * steps : (band + 1) * steps].reshape(steps * shots, receivers)
        sums = shot_sums(lines, aperture, shot_weight)
        columns[band] = subtract_waves(band, sums, waves)
    tiles_turned[...] = tiles_near[...].astype(F32).T.astype(BF16)
    kind = lax.broadcasted_iota(jnp.int32, chosen.shape, 0)
    chosen[...] = jnp.where(kinds[...] == kind, 1.0, 0.0)
    send[...] = theirs[...]


def column_kernel(columns, got, *refs):
    total = refs[-1]
    col = lax.axis_index("col")
    waves = got[...].astype(F32)
    for band in range(columns.shape[0]):
        total[band] = subtract_waves(band, columns[band], waves)
    for offset, out in enumerate(refs[:-1]):
        out[...] = total[col ^ offset].astype(out.dtype)


def primaries_kernel(mine, got, held, out, token):
    samples, shots, receivers = held.shape
    rows = 16
    for start in range(0, shots, rows):
        here = slice(start, start + rows)
        parts = []
        for freq in range(NF):
            both = mine[freq, here].astype(F32) + got[freq, here].astype(F32)
            parts += [both[:, :receivers], both[:, receivers:]]
        for sample in range(HALF_TURN):
            wave = weighted_sum(wave_weights(sample), parts)
            for turn in range(samples // HALF_TURN):
                at = sample + turn * HALF_TURN
                trace = held[at, here].astype(F32)
                out[at, here] = (trace + wave if turn % 2 else trace - wave).astype(BF16)
    token[...] = jnp.zeros_like(token)


def image_kernel(shots, bands, *refs):
    parts = refs[:bands]
    tiles_turned, chosen, _, image = refs[bands:]
    total = parts[0][...]
    for part in parts[1:]:
        total = total + part[...].astype(F32)
    column_stack = total / math.sqrt(shots)
    steps, panel = column_stack.shape
    kinds = chosen.shape[0]
    rounded = column_stack.astype(BF16).astype(F32)
    widened = jnp.where(chosen[...][:, None, :] > 0.5, rounded[None], 0.0)
    image[...] = dot(tiles_turned[...], widened.reshape(kinds * steps, panel).astype(BF16))


WHOLE = pl.BlockSpec(memory_space=pltpu.VMEM)
IN_HBM = pl.BlockSpec(memory_space=pltpu.HBM)


def in_vmem(*arrays):
    return [pltpu.with_memory_space_constraint(a, pltpu.VMEM) for a in arrays]


def in_hbm(*arrays):
    return [pltpu.with_memory_space_constraint(a, pltpu.HBM) for a in arrays]


def call(body, out_shape, in_specs, out_specs, scratch=(), flops=0, moved=0):
    return pl.pallas_call(
        body,
        out_shape=out_shape,
        in_specs=in_specs,
        out_specs=out_specs,
        scratch_shapes=list(scratch),
        compiler_params=pltpu.CompilerParams(vmem_limit_bytes=VMEM_BYTES),
        cost_estimate=pl.CostEstimate(flops=flops, bytes_accessed=moved, transcendentals=0),
    )


def swap(array, axis, size, offset):
    return lax.ppermute(array, axis, [(i, i ^ offset) for i in range(size)])


def per_device(traces, source_pos, receiver_pos, aperture_list, band_index, weight_tiles):
    samples, shots, receivers = traces.shape
    rows, cols = lax.axis_size("row"), lax.axis_size("col")
    panel = band_index.shape[0]
    steps = samples // cols
    kinds, _, depth = weight_tiles.shape
    spread_len = float(panel * rows // 4)
    levels = rows // 2
    tiles, listed = aperture_list.shape
    assert receivers == 2 * shots and levels == cols

    plane_shape = (NF, 2, shots, receivers)
    half_shape = (NF, shots, receivers)
    part = pltpu.VMEM((NF, shots, 2 * receivers), BF16)
    extra = digit_rows(tiles, listed)
    table = pltpu.VMEM((receivers, panel), BF16)
    weights = pltpu.VMEM((shots, panel), F32)
    held, planes, mine, theirs, lists, places, stations, near_kinds, tiles_near = call(
        spectra_kernel,
        [
            pltpu.VMEM(traces.shape, BF16),
            pltpu.VMEM(plane_shape, BF16),
            pltpu.VMEM(half_shape, BF16),
            pltpu.VMEM((NF * shots + extra, receivers), BF16),
            pltpu.VMEM(aperture_list.shape, jnp.int32),
            pltpu.VMEM((1, shots), jnp.int32),
            pltpu.VMEM((cols, receivers), jnp.int32),
            pltpu.VMEM((1, panel), jnp.int32),
            pltpu.VMEM((kinds * steps, depth), BF16),
        ],
        [IN_HBM] * 6,
        [WHOLE] * 9,
        [
            pltpu.VMEM((2,) + half_shape, BF16),
            pltpu.VMEM((extra, DIGIT), F32),
            pltpu.SemaphoreType.DMA((PARTS + 5,)),
        ],
    )(
        *in_hbm(
            traces,
            aperture_list,
            source_pos.reshape(1, shots),
            receiver_pos.reshape(cols, receivers),
            band_index.reshape(1, panel),
            weight_tiles.reshape(kinds * steps, depth),
        )
    )
    rights = [planes] + [
        lax.ppermute(planes, "row", [(2 * a + x, 2 * b + x) for a, b in enumerate(to) for x in range(2)])
        for to in routes(levels)
    ]
    got = swap(theirs, "row", rows, 1)
    both = call(pair_kernel, pltpu.VMEM((2,) + half_shape, BF16), [WHOLE] * 2, WHOLE)(
        *in_vmem(mine, got)
    )
    left = lax.all_gather(both, "col")
    aperture, shot_weight, their_aperture, their_weight = call(
        functools.partial(tables_kernel, spread_len),
        [table, weights] * 2,
        [WHOLE] * 5,
        [WHOLE] * 4,
        [pltpu.VMEM((extra, DIGIT), F32)],
    )(*in_vmem(left, got, lists, places, stations))
    theirs, waves = call(
        functools.partial(product_kernel, levels),
        [part, pltpu.VMEM((HALF_TURN, panel), LINKT)],
        [WHOLE] * (levels + 3),
        [WHOLE] * 2,
    )(*in_vmem(left, *rights, their_aperture, their_weight))
    got_waves = swap(waves, "row", rows, 1)
    mine, columns, tiles_turned, chosen, send = call(
        functools.partial(own_stack_kernel, levels),
        [
            part,
            pltpu.VMEM((cols, steps, panel), F32),
            pltpu.VMEM((depth, kinds * steps), BF16),
            pltpu.VMEM((kinds, panel), F32),
            part,
        ],
        [WHOLE] * (levels + 7),
        [WHOLE] * 5,
        flops=1 << 34,
    )(*in_vmem(left, *rights, theirs, held, aperture, shot_weight, near_kinds, tiles_near))
    got_part = swap(send, "row", rows, 1)
    band = pltpu.VMEM((steps, panel), F32)
    own, *sends = call(
        column_kernel,
        [band] + [pltpu.VMEM((steps, panel), LINKT)] * (cols - 1),
        [WHOLE] * 2,
        [WHOLE] * cols,
        [pltpu.VMEM((cols, steps, panel), F32)],
        flops=1 << 34,
    )(*in_vmem(columns, got_waves))
    order = list(range(cols - 1))[::-1]
    bands = [own] + [swap(sends[d], "col", cols, d + 1) for d in order]
    primaries, token = call(
        primaries_kernel,
        [pltpu.VMEM(traces.shape, BF16), pltpu.VMEM((8, 128), F32)],
        [WHOLE] * 3,
        [WHOLE] * 2,
        flops=1 << 20,
        moved=3 << 20,
    )(*in_vmem(mine, got_part, held))
    image = call(
        functools.partial(image_kernel, shots, cols),
        jax.ShapeDtypeStruct((depth, panel), F32),
        [WHOLE] * (cols + 3),
        WHOLE,
    )(*in_vmem(*bands, tiles_turned, chosen, token))
    return primaries, image


def solution(mesh):
    placed = (P(None, "row", "col"), P("row"), P(), P("row", None), P("row"), P())
    return jax.shard_map(
        per_device,
        mesh=mesh,
        in_specs=placed,
        out_specs=(P(None, "row", "col"), P("col", "row")),
        check_vma=False,
    )
```

```python
import functools
import math

import jax
import jax.numpy as jnp
import ml_dtypes
import numpy as np
from jax import lax
from jax.experimental import pallas as pl
from jax.experimental.pallas import tpu as pltpu
from jax.sharding import PartitionSpec as P

NFFT = 4096
NF = 4
STEP = NFFT // (4 * NF)
HALF_TURN = NFFT // (2 * STEP)
F32 = jnp.float32
BF16 = jnp.bfloat16
PARTS = 2


def routes(levels):
    if levels == 4:
        return [[2, 3, 1, 0], [1, 0, 3, 2], [3, 2, 0, 1]]
    return [[(a + d) % levels for a in range(levels)] for d in range(1, levels)]


LINKT = BF16
VMEM_BYTES = 48 * 1024 * 1024


def angle(freq, sample):
    return 2.0 * math.pi * (((2 * freq + 1) * STEP * sample) % NFFT) / NFFT


def forward_weight(freq, part, sample, samples):
    value = (math.cos, lambda a: -math.sin(a))[part](angle(freq, sample)) / math.sqrt(samples)
    return float(np.float32(value).astype(ml_dtypes.bfloat16)) if abs(value) > 1e-6 else 0.0


def weighted_sum(weights, arrays):
    total = None
    for weight, array in zip(weights, arrays):
        if abs(weight) > 1e-6:
            total = weight * array if total is None else total + weight * array
    return total


def dot(left, right):
    return jnp.dot(left, right, preferred_element_type=F32)


def wave_weights(sample):
    weights = []
    for freq in range(NF):
        weights += [math.cos(angle(freq, sample)), -math.sin(angle(freq, sample))]
    return [w / math.sqrt(NF) for w in weights]


DIGIT = 128


def digit_rows(tiles, listed):
    used = 2 * tiles * (listed // DIGIT) + 2
    return -(-used // 16) * 16


def upright(line):
    length = line.shape[1]
    at_row = lax.broadcasted_iota(jnp.int32, (length, length), 0)
    at_lane = lax.broadcasted_iota(jnp.int32, (length, length), 1)
    return jnp.sum(jnp.where(at_row == at_lane, line.astype(F32), 0.0), axis=1, keepdims=True)


def taper(positions, panel, first, spread_len):
    columns = (lax.broadcasted_iota(jnp.int32, (positions.shape[0], panel), 1) + first).astype(F32)
    offset = (positions - columns) / spread_len
    return 1.0 / (1.0 + offset * offset)


def fill_aperture(aperture, listing, near):
    receivers, panel = aperture.shape
    tiles, listed = listing.shape
    width = panel // tiles
    receiver = lax.broadcasted_iota(jnp.int32, (receivers, listed), 0)
    receiver = (receiver + lax.axis_index("col") * receivers).astype(F32)
    ones = jnp.ones((listed, width), BF16)
    for tile in range(tiles):
        hits = jnp.where(listing[tile : tile + 1] == receiver, 1.0, 0.0).astype(BF16)
        here = slice(tile * width, (tile + 1) * width)
        weighted = dot(hits, ones) * near[:, here] * (2.0 / math.sqrt(listed))
        aperture[:, here] = weighted.astype(BF16)


def spectra_kernel(
    traces, aperture_list, source_pos, receiver_pos, band_index, weight_tiles,
    held, planes, mine, theirs, lists, places, stations, kinds, tiles_near,
    halves, digits, arrived,
):
    samples, shots, receivers = held.shape
    rows = shots // PARTS
    copies = []
    for part in range(PARTS):
        piece = (slice(None), pl.ds(part * rows, rows))
        copies.append(pltpu.make_async_copy(traces.at[piece], held.at[piece], arrived.at[part]))
    given = (aperture_list, source_pos, receiver_pos, band_index, weight_tiles)
    for index, near in enumerate((lists, places, stations, kinds, tiles_near)):
        copies.append(pltpu.make_async_copy(given[index], near, arrived.at[PARTS + index]))
    for copy in copies:
        copy.start()
    lane = lax.broadcasted_iota(jnp.int32, (rows, receivers), 1)
    low = lane < receivers // 2
    for part in range(PARTS):
        copies[part].wait()
        here = slice(part * rows, (part + 1) * rows)
        folded = []
        for sample in range(HALF_TURN):
            total = held[sample, here].astype(F32)
            for turn in range(1, samples // HALF_TURN):
                term = held[sample + turn * HALF_TURN, here].astype(F32)
                total = total - term if turn % 2 else total + term
            folded.append(total)
        for freq in range(NF):
            pair = []
            for piece in range(2):
                weights = [forward_weight(freq, piece, t, samples) for t in range(HALF_TURN)]
                pair.append(weighted_sum(weights, folded))
                planes[freq, piece, here] = pair[piece].astype(BF16)
            real, imag = pair
            turned = [pltpu.roll(p, receivers // 2, 1) for p in pair]
            halves[0, freq, here] = jnp.where(low, real, turned[1]).astype(BF16)
            halves[1, freq, here] = jnp.where(low, turned[0], imag).astype(BF16)
    for copy in copies[PARTS:]:
        copy.wait()
    tiles, listed = lists.shape
    groups = listed // DIGIT
    digits[...] = jnp.zeros_like(digits)
    for group in range(groups):
        some = lists[:, group * DIGIT : (group + 1) * DIGIT]
        start = 2 * group * tiles
        digits[start : start + tiles] = (some >> 7).astype(F32)
        digits[start + tiles : start + 2 * tiles] = (some & (DIGIT - 1)).astype(F32)
    start = 2 * groups * tiles
    digits[start : start + 1, 0:shots] = (places[...] >> 7).astype(F32)
    digits[start + 1 : start + 2, 0:shots] = (places[...] & (DIGIT - 1)).astype(F32)
    side = lax.rem(lax.axis_index("row"), 2)
    mine[...] = halves[side]
    theirs[0 : NF * shots] = halves[1 - side].reshape(NF * shots, receivers)
    theirs[NF * shots :] = digits[...].astype(BF16)


def pair_kernel(mine, got, both):
    both[0] = mine[...]
    both[1] = got[0 : mine.shape[0] * mine.shape[1]].reshape(mine.shape)


def shot_sums(lines, aperture, shot_weight):
    shots, panel = shot_weight.shape
    stacked = dot(lines, aperture[...]).reshape(lines.shape[0] // shots, shots, panel)
    return jnp.sum(stacked * shot_weight[...][None], axis=1)


def panel_stack(parts, aperture, shot_weight):
    receivers = aperture.shape[0]
    both = parts[...]
    lines = jnp.concatenate(
        [both[freq][:, lanes] for freq in range(NF) for lanes in (slice(0, receivers), slice(receivers, None))]
    )
    sums = shot_sums(lines, aperture, shot_weight)
    rows = [sums[k : k + 1] for k in range(2 * NF)]
    waves = [weighted_sum(wave_weights(sample), rows) for sample in range(HALF_TURN)]
    return jnp.concatenate(waves, axis=0)


def level_blocks(rights, levels):
    level = lax.axis_index("row") // 2
    blocks = [(level, rights[0])]
    for to, got in zip(routes(levels), rights[1:]):
        blocks.append((sum(jnp.where(level == there, here, 0) for here, there in enumerate(to)), got))
    return blocks


def product(part, freq, left, blocks):
    step = min(2, len(blocks))
    total = None
    for first in range(0, len(blocks), step):
        some = blocks[first : first + step]
        near = jnp.concatenate([left[origin, part, freq] for origin, _ in some], axis=1)
        far = []
        for _, right in some:
            real, imag = right[freq, 0], right[freq, 1]
            far.append(jnp.concatenate([real, imag], axis=1))
            far.append(jnp.concatenate([-imag, real], axis=1))
        term = dot(near, jnp.concatenate(far, axis=0))
        total = term if total is None else total + term
    surface = 2 * len(blocks) * left.shape[3]
    return (total * (-1.0 / math.sqrt(surface))).astype(BF16)


def product_kernel(levels, left, *refs):
    aperture, shot_weight, theirs, waves = refs[levels:]
    blocks = level_blocks(refs[:levels], levels)
    for freq in range(NF):
        theirs[freq] = product(1, freq, left, blocks)
    waves[...] = panel_stack(theirs, aperture, shot_weight).astype(waves.dtype)


def tables_kernel(
    spread_len, left, got, lists, places, stations, aperture, shot_weight, their_aperture, their_weight, digits
):
    del left
    shots, panel = shot_weight.shape
    tiles, listed = lists.shape
    row, col = lax.axis_index("row"), lax.axis_index("col")
    digits[...] = got[NF * shots :].astype(F32)
    listing = []
    start = 0
    for _ in range(listed // DIGIT):
        high, low = digits[start : start + tiles], digits[start + tiles : start + 2 * tiles]
        listing.append(high * DIGIT + low)
        start += 2 * tiles
    there = digits[start : start + 1, 0:shots] * DIGIT + digits[start + 1 : start + 2, 0:shots]
    position = upright(stations[pl.ds(col, 1)])
    for first, some, sources, table, weight in (
        (row * panel, lists[...].astype(F32), places[...], aperture, shot_weight),
        ((row ^ 1) * panel, jnp.concatenate(listing, axis=1), there, their_aperture, their_weight),
    ):
        fill_aperture(table, some, taper(position, panel, first, spread_len))
        weight[...] = taper(upright(sources), panel, first, spread_len)


def subtract_waves(band, columns, waves):
    steps = columns.shape[0]
    start = band * steps
    sign = -1.0 if (start // HALF_TURN) % 2 else 1.0
    first = start % HALF_TURN
    return columns - sign * waves[first : first + steps]


def own_stack_kernel(levels, left, *refs):
    (
        held, aperture, shot_weight, kinds, tiles_near,
        mine, columns, tiles_turned, chosen,
    ) = refs[levels:]
    blocks = level_blocks(refs[:levels], levels)
    for freq in range(NF):
        mine[freq] = product(0, freq, left, blocks)
    waves = panel_stack(mine, aperture, shot_weight)
    bands, steps, _ = columns.shape
    _, shots, receivers = held.shape
    for band in range(bands):
        lines = held[band * steps : (band + 1) * steps].reshape(steps * shots, receivers)
        sums = shot_sums(lines, aperture, shot_weight)
        columns[band] = subtract_waves(band, sums, waves)
    tiles_turned[...] = tiles_near[...].astype(F32).T.astype(BF16)
    kind = lax.broadcasted_iota(jnp.int32, chosen.shape, 0)
    chosen[...] = jnp.where(kinds[...][:, None, :] == kind, 1.0, 0.0)


def column_kernel(columns, got, *refs):
    total = refs[-1]
    col = lax.axis_index("col")
    waves = got[...].astype(F32)
    for band in range(columns.shape[0]):
        total[band] = subtract_waves(band, columns[band], waves)
    for offset, out in enumerate(refs[:-1]):
        out[...] = total[col ^ offset].astype(out.dtype)


def primaries_kernel(mine, got, held, out, token):
    samples, shots, receivers = held.shape
    rows = 16
    for start in range(0, shots, rows):
        here = slice(start, start + rows)
        parts = []
        for freq in range(NF):
            both = mine[freq, here].astype(F32) + got[freq, here].astype(F32)
            parts += [both[:, :receivers], both[:, receivers:]]
        for sample in range(HALF_TURN):
            wave = weighted_sum(wave_weights(sample), parts)
            for turn in range(samples // HALF_TURN):
                at = sample + turn * HALF_TURN
                trace = held[at, here].astype(F32)
                out[at, here] = (trace + wave if turn % 2 else trace - wave).astype(BF16)
    token[...] = jnp.zeros_like(token)


def image_kernel(shots, bands, *refs):
    parts = refs[:bands]
    tiles_turned, chosen, _, image = refs[bands:]
    total = parts[0][...]
    for part in parts[1:]:
        total = total + part[...].astype(F32)
    column_stack = total / math.sqrt(shots)
    steps, panel = column_stack.shape
    kinds = chosen.shape[0]
    rounded = column_stack.astype(BF16).astype(F32)
    widened = jnp.where(chosen[...] > 0.5, rounded[None], 0.0)
    image[...] = dot(tiles_turned[...], widened.reshape(kinds * steps, panel).astype(BF16))


WHOLE = pl.BlockSpec(memory_space=pltpu.VMEM)
IN_HBM = pl.BlockSpec(memory_space=pltpu.HBM)


def in_vmem(*arrays):
    return [pltpu.with_memory_space_constraint(a, pltpu.VMEM) for a in arrays]


def in_hbm(*arrays):
    return [pltpu.with_memory_space_constraint(a, pltpu.HBM) for a in arrays]


def call(body, out_shape, in_specs, out_specs, scratch=(), flops=0, moved=0):
    return pl.pallas_call(
        body,
        out_shape=out_shape,
        in_specs=in_specs,
        out_specs=out_specs,
        scratch_shapes=list(scratch),
        compiler_params=pltpu.CompilerParams(vmem_limit_bytes=VMEM_BYTES),
        cost_estimate=pl.CostEstimate(flops=flops, bytes_accessed=moved, transcendentals=0),
    )


def swap(array, axis, size, offset):
    return lax.ppermute(array, axis, [(i, i ^ offset) for i in range(size)])


def per_device(traces, source_pos, receiver_pos, aperture_list, band_index, weight_tiles):
    samples, shots, receivers = traces.shape
    rows, cols = lax.axis_size("row"), lax.axis_size("col")
    panel = band_index.shape[0]
    steps = samples // cols
    kinds, _, depth = weight_tiles.shape
    spread_len = float(panel * rows // 4)
    levels = rows // 2
    tiles, listed = aperture_list.shape
    assert receivers == 2 * shots and levels == cols

    plane_shape = (NF, 2, shots, receivers)
    half_shape = (NF, shots, receivers)
    part = pltpu.VMEM((NF, shots, 2 * receivers), BF16)
    extra = digit_rows(tiles, listed)
    table = pltpu.VMEM((receivers, panel), BF16)
    weights = pltpu.VMEM((shots, panel), F32)
    held, planes, mine, theirs, lists, places, stations, near_kinds, tiles_near = call(
        spectra_kernel,
        [
            pltpu.VMEM(traces.shape, BF16),
            pltpu.VMEM(plane_shape, BF16),
            pltpu.VMEM(half_shape, BF16),
            pltpu.VMEM((NF * shots + extra, receivers), BF16),
            pltpu.VMEM(aperture_list.shape, jnp.int32),
            pltpu.VMEM((1, shots), jnp.int32),
            pltpu.VMEM((cols, receivers), jnp.int32),
            pltpu.VMEM((1, panel), jnp.int32),
            pltpu.VMEM((kinds * steps, depth), BF16),
        ],
        [IN_HBM] * 6,
        [WHOLE] * 9,
        [
            pltpu.VMEM((2,) + half_shape, BF16),
            pltpu.VMEM((extra, DIGIT), F32),
            pltpu.SemaphoreType.DMA((PARTS + 5,)),
        ],
    )(
        *in_hbm(
            traces,
            aperture_list,
            source_pos.reshape(1, shots),
            receiver_pos.reshape(cols, receivers),
            band_index.reshape(1, panel),
            weight_tiles.reshape(kinds * steps, depth),
        )
    )
    rights = [planes] + [
        lax.ppermute(planes, "row", [(2 * a + x, 2 * b + x) for a, b in enumerate(to) for x in range(2)])
        for to in routes(levels)
    ]
    got = swap(theirs, "row", rows, 1)
    both = call(pair_kernel, pltpu.VMEM((2,) + half_shape, BF16), [WHOLE] * 2, WHOLE)(
        *in_vmem(mine, got)
    )
    left = lax.all_gather(both, "col")
    aperture, shot_weight, their_aperture, their_weight = call(
        functools.partial(tables_kernel, spread_len),
        [table, weights] * 2,
        [WHOLE] * 5,
        [WHOLE] * 4,
        [pltpu.VMEM((extra, DIGIT), F32)],
    )(*in_vmem(left, got, lists, places, stations))
    theirs, waves = call(
        functools.partial(product_kernel, levels),
        [part, pltpu.VMEM((HALF_TURN, panel), LINKT)],
        [WHOLE] * (levels + 3),
        [WHOLE] * 2,
    )(*in_vmem(left, *rights, their_aperture, their_weight))
    got_waves = swap(waves, "row", rows, 1)
    mine, columns, tiles_turned, chosen = call(
        functools.partial(own_stack_kernel, levels),
        [
            part,
            pltpu.VMEM((cols, steps, panel), F32),
            pltpu.VMEM((depth, kinds * steps), BF16),
            pltpu.VMEM((kinds, steps, panel), F32),
        ],
        [WHOLE] * (levels + 6),
        [WHOLE] * 4,
        flops=1 << 34,
    )(*in_vmem(left, *rights, held, aperture, shot_weight, near_kinds, tiles_near))
    got_part = swap(theirs, "row", rows, 1)
    band = pltpu.VMEM((steps, panel), F32)
    own, *sends = call(
        column_kernel,
        [band] + [pltpu.VMEM((steps, panel), LINKT)] * (cols - 1),
        [WHOLE] * 2,
        [WHOLE] * cols,
        [pltpu.VMEM((cols, steps, panel), F32)],
        flops=1 << 34,
    )(*in_vmem(columns, got_waves))
    order = list(range(cols - 1))[::-1]
    bands = [own] + [swap(sends[d], "col", cols, d + 1) for d in order]
    primaries, token = call(
        primaries_kernel,
        [pltpu.VMEM(traces.shape, BF16), pltpu.VMEM((8, 128), F32)],
        [WHOLE] * 3,
        [WHOLE] * 2,
        flops=1 << 20,
        moved=3 << 20,
    )(*in_vmem(mine, got_part, held))
    image = call(
        functools.partial(image_kernel, shots, cols),
        jax.ShapeDtypeStruct((depth, panel), F32),
        [WHOLE] * (cols + 3),
        WHOLE,
    )(*in_vmem(*bands, tiles_turned, chosen, token))
    return primaries, image


def solution(mesh):
    placed = (P(None, "row", "col"), P("row"), P(), P("row", None), P("row"), P())
    return jax.shard_map(
        per_device,
        mesh=mesh,
        in_specs=placed,
        out_specs=(P(None, "row", "col"), P("col", "row")),
        check_vma=False,
    )
```

```python
import functools
import math

import jax
import jax.numpy as jnp
import ml_dtypes
import numpy as np
from jax import lax
from jax.experimental import pallas as pl
from jax.experimental.pallas import tpu as pltpu
from jax.sharding import PartitionSpec as P

NFFT = 4096
NF = 4
STEP = NFFT // (4 * NF)
HALF_TURN = NFFT // (2 * STEP)
F32 = jnp.float32
BF16 = jnp.bfloat16
PARTS = 2


def routes(levels):
    if levels == 4:
        return [[2, 3, 1, 0], [1, 0, 3, 2], [3, 2, 0, 1]]
    return [[(a + d) % levels for a in range(levels)] for d in range(1, levels)]


LINKT = BF16
VMEM_BYTES = 48 * 1024 * 1024


def angle(freq, sample):
    return 2.0 * math.pi * (((2 * freq + 1) * STEP * sample) % NFFT) / NFFT


def forward_weight(freq, part, sample, samples):
    value = (math.cos, lambda a: -math.sin(a))[part](angle(freq, sample)) / math.sqrt(samples)
    return float(np.float32(value).astype(ml_dtypes.bfloat16)) if abs(value) > 1e-6 else 0.0


def weighted_sum(weights, arrays):
    total = None
    for weight, array in zip(weights, arrays):
        if abs(weight) > 1e-6:
            total = weight * array if total is None else total + weight * array
    return total


def dot(left, right):
    return jnp.dot(left, right, preferred_element_type=F32)


def wave_weights(sample):
    weights = []
    for freq in range(NF):
        weights += [math.cos(angle(freq, sample)), -math.sin(angle(freq, sample))]
    return [w / math.sqrt(NF) for w in weights]


DIGIT = 128


def digit_rows(tiles, listed):
    used = 2 * tiles * (listed // DIGIT) + 2
    return -(-used // 16) * 16


def upright(line):
    length = line.shape[1]
    at_row = lax.broadcasted_iota(jnp.int32, (length, length), 0)
    at_lane = lax.broadcasted_iota(jnp.int32, (length, length), 1)
    return jnp.sum(jnp.where(at_row == at_lane, line.astype(F32), 0.0), axis=1, keepdims=True)


def taper(positions, panel, first, spread_len):
    columns = (lax.broadcasted_iota(jnp.int32, (positions.shape[0], panel), 1) + first).astype(F32)
    offset = (positions - columns) / spread_len
    return 1.0 / (1.0 + offset * offset)


def fill_aperture(aperture, listing, near):
    receivers, panel = aperture.shape
    tiles, listed = listing.shape
    width = panel // tiles
    receiver = lax.broadcasted_iota(jnp.int32, (receivers, listed), 0)
    receiver = (receiver + lax.axis_index("col") * receivers).astype(F32)
    ones = jnp.ones((listed, width), BF16)
    for tile in range(tiles):
        hits = jnp.where(listing[tile : tile + 1] == receiver, 1.0, 0.0).astype(BF16)
        here = slice(tile * width, (tile + 1) * width)
        weighted = dot(hits, ones) * near[:, here] * (2.0 / math.sqrt(listed))
        aperture[:, here] = weighted.astype(BF16)


def spectra_kernel(
    traces, aperture_list, source_pos, receiver_pos, band_index, weight_tiles,
    held, planes, mine, theirs, lists, places, stations, kinds, tiles_near,
    halves, digits, arrived,
):
    samples, shots, receivers = held.shape
    rows = shots // PARTS
    copies = []
    for part in range(PARTS):
        piece = (slice(None), pl.ds(part * rows, rows))
        copies.append(pltpu.make_async_copy(traces.at[piece], held.at[piece], arrived.at[part]))
    given = (aperture_list, source_pos, receiver_pos, band_index, weight_tiles)
    for index, near in enumerate((lists, places, stations, kinds, tiles_near)):
        copies.append(pltpu.make_async_copy(given[index], near, arrived.at[PARTS + index]))
    for copy in copies:
        copy.start()
    lane = lax.broadcasted_iota(jnp.int32, (rows, receivers), 1)
    low = lane < receivers // 2
    for part in range(PARTS):
        copies[part].wait()
        here = slice(part * rows, (part + 1) * rows)
        folded = []
        for sample in range(HALF_TURN):
            total = held[sample, here].astype(F32)
            for turn in range(1, samples // HALF_TURN):
                term = held[sample + turn * HALF_TURN, here].astype(F32)
                total = total - term if turn % 2 else total + term
            folded.append(total)
        pairs = [[None, None] for _ in range(NF)]
        for freq in range(NF // 2):
            for piece in range(2):
                weights = [forward_weight(freq, piece, t, samples) for t in range(HALF_TURN)]
                even = weighted_sum(weights[0::2], folded[0::2])
                odd = weighted_sum(weights[1::2], folded[1::2])
                pairs[freq][piece] = even + odd
                pairs[NF - 1 - freq][piece] = odd - even if piece else even - odd
        for freq in range(NF):
            pair = pairs[freq]
            for piece in range(2):
                planes[freq, piece, here] = pair[piece].astype(BF16)
            real, imag = pair
            turned = [pltpu.roll(p, receivers // 2, 1) for p in pair]
            halves[0, freq, here] = jnp.where(low, real, turned[1]).astype(BF16)
            halves[1, freq, here] = jnp.where(low, turned[0], imag).astype(BF16)
    for copy in copies[PARTS:]:
        copy.wait()
    tiles, listed = lists.shape
    groups = listed // DIGIT
    digits[...] = jnp.zeros_like(digits)
    for group in range(groups):
        some = lists[:, group * DIGIT : (group + 1) * DIGIT]
        start = 2 * group * tiles
        digits[start : start + tiles] = (some >> 7).astype(F32)
        digits[start + tiles : start + 2 * tiles] = (some & (DIGIT - 1)).astype(F32)
    start = 2 * groups * tiles
    digits[start : start + 1, 0:shots] = (places[...] >> 7).astype(F32)
    digits[start + 1 : start + 2, 0:shots] = (places[...] & (DIGIT - 1)).astype(F32)
    side = lax.rem(lax.axis_index("row"), 2)
    mine[...] = halves[side]
    theirs[0 : NF * shots] = halves[1 - side].reshape(NF * shots, receivers)
    theirs[NF * shots :] = digits[...].astype(BF16)


def pair_kernel(mine, got, both):
    both[0] = mine[...]
    both[1] = got[0 : mine.shape[0] * mine.shape[1]].reshape(mine.shape)


def shot_sums(lines, aperture, shot_weight):
    shots, panel = shot_weight.shape
    stacked = dot(lines, aperture[...]).reshape(lines.shape[0] // shots, shots, panel)
    return jnp.sum(stacked * shot_weight[...][None], axis=1)


def panel_stack(parts, aperture, shot_weight):
    receivers = aperture.shape[0]
    both = parts[...]
    lines = jnp.concatenate(
        [both[freq][:, lanes] for freq in range(NF) for lanes in (slice(0, receivers), slice(receivers, None))]
    )
    sums = shot_sums(lines, aperture, shot_weight)
    rows = [sums[k : k + 1] for k in range(2 * NF)]
    waves = [weighted_sum(wave_weights(sample), rows) for sample in range(HALF_TURN)]
    return jnp.concatenate(waves, axis=0)


def level_blocks(rights, levels):
    level = lax.axis_index("row") // 2
    blocks = [(level, rights[0])]
    for to, got in zip(routes(levels), rights[1:]):
        blocks.append((sum(jnp.where(level == there, here, 0) for here, there in enumerate(to)), got))
    return blocks


def product(part, freq, left, blocks):
    step = min(2, len(blocks))
    total = None
    for first in range(0, len(blocks), step):
        some = blocks[first : first + step]
        near = jnp.concatenate([left[origin, part, freq] for origin, _ in some], axis=1)
        far = []
        for _, right in some:
            real, imag = right[freq, 0], right[freq, 1]
            far.append(jnp.concatenate([real, imag], axis=1))
            far.append(jnp.concatenate([-imag, real], axis=1))
        term = dot(near, jnp.concatenate(far, axis=0))
        total = term if total is None else total + term
    surface = 2 * len(blocks) * left.shape[3]
    return (total * (-1.0 / math.sqrt(surface))).astype(BF16)


def product_kernel(levels, left, *refs):
    aperture, shot_weight, theirs, waves = refs[levels:]
    blocks = level_blocks(refs[:levels], levels)
    for freq in range(NF):
        theirs[freq] = product(1, freq, left, blocks)
    waves[...] = panel_stack(theirs, aperture, shot_weight).astype(waves.dtype)


def tables_kernel(
    spread_len, left, got, lists, places, stations, aperture, shot_weight, their_aperture, their_weight, digits
):
    del left
    shots, panel = shot_weight.shape
    tiles, listed = lists.shape
    row, col = lax.axis_index("row"), lax.axis_index("col")
    digits[...] = got[NF * shots :].astype(F32)
    listing = []
    start = 0
    for _ in range(listed // DIGIT):
        high, low = digits[start : start + tiles], digits[start + tiles : start + 2 * tiles]
        listing.append(high * DIGIT + low)
        start += 2 * tiles
    there = digits[start : start + 1, 0:shots] * DIGIT + digits[start + 1 : start + 2, 0:shots]
    position = upright(stations[pl.ds(col, 1)])
    for first, some, sources, table, weight in (
        (row * panel, lists[...].astype(F32), places[...], aperture, shot_weight),
        ((row ^ 1) * panel, jnp.concatenate(listing, axis=1), there, their_aperture, their_weight),
    ):
        fill_aperture(table, some, taper(position, panel, first, spread_len))
        weight[...] = taper(upright(sources), panel, first, spread_len)


def subtract_waves(band, columns, waves):
    steps = columns.shape[0]
    start = band * steps
    sign = -1.0 if (start // HALF_TURN) % 2 else 1.0
    first = start % HALF_TURN
    return columns - sign * waves[first : first + steps]


def own_stack_kernel(levels, left, *refs):
    (
        held, aperture, shot_weight, kinds, tiles_near,
        mine, columns, tiles_turned, chosen,
    ) = refs[levels:]
    blocks = level_blocks(refs[:levels], levels)
    for freq in range(NF):
        mine[freq] = product(0, freq, left, blocks)
    waves = panel_stack(mine, aperture, shot_weight)
    bands, steps, _ = columns.shape
    _, shots, receivers = held.shape
    for band in range(bands):
        lines = held[band * steps : (band + 1) * steps].reshape(steps * shots, receivers)
        sums = shot_sums(lines, aperture, shot_weight)
        columns[band] = subtract_waves(band, sums, waves)
    tiles_turned[...] = tiles_near[...].astype(F32).T.astype(BF16)
    kind = lax.broadcasted_iota(jnp.int32, chosen.shape, 0)
    chosen[...] = jnp.where(kinds[...][:, None, :] == kind, 1.0, 0.0)


def column_kernel(columns, got, *refs):
    total = refs[-1]
    col = lax.axis_index("col")
    waves = got[...].astype(F32)
    for band in range(columns.shape[0]):
        total[band] = subtract_waves(band, columns[band], waves)
    for offset, out in enumerate(refs[:-1]):
        out[...] = total[col ^ offset].astype(out.dtype)


def primaries_kernel(mine, got, held, out, token):
    samples, shots, receivers = held.shape
    rows = 16
    for start in range(0, shots, rows):
        here = slice(start, start + rows)
        parts = []
        for freq in range(NF):
            both = mine[freq, here].astype(F32) + got[freq, here].astype(F32)
            parts += [both[:, :receivers], both[:, receivers:]]
        for sample in range(HALF_TURN):
            wave = weighted_sum(wave_weights(sample), parts)
            for turn in range(samples // HALF_TURN):
                at = sample + turn * HALF_TURN
                trace = held[at, here].astype(F32)
                out[at, here] = (trace + wave if turn % 2 else trace - wave).astype(BF16)
    token[...] = jnp.zeros_like(token)


def image_kernel(shots, bands, *refs):
    parts = refs[:bands]
    tiles_turned, chosen, _, image = refs[bands:]
    total = parts[0][...]
    for part in parts[1:]:
        total = total + part[...].astype(F32)
    column_stack = total / math.sqrt(shots)
    steps, panel = column_stack.shape
    kinds = chosen.shape[0]
    rounded = column_stack.astype(BF16).astype(F32)
    widened = jnp.where(chosen[...] > 0.5, rounded[None], 0.0)
    image[...] = dot(tiles_turned[...], widened.reshape(kinds * steps, panel).astype(BF16))


WHOLE = pl.BlockSpec(memory_space=pltpu.VMEM)
IN_HBM = pl.BlockSpec(memory_space=pltpu.HBM)


def in_vmem(*arrays):
    return [pltpu.with_memory_space_constraint(a, pltpu.VMEM) for a in arrays]


def in_hbm(*arrays):
    return [pltpu.with_memory_space_constraint(a, pltpu.HBM) for a in arrays]


def call(body, out_shape, in_specs, out_specs, scratch=(), flops=0, moved=0):
    return pl.pallas_call(
        body,
        out_shape=out_shape,
        in_specs=in_specs,
        out_specs=out_specs,
        scratch_shapes=list(scratch),
        compiler_params=pltpu.CompilerParams(vmem_limit_bytes=VMEM_BYTES),
        cost_estimate=pl.CostEstimate(flops=flops, bytes_accessed=moved, transcendentals=0),
    )


def swap(array, axis, size, offset):
    return lax.ppermute(array, axis, [(i, i ^ offset) for i in range(size)])


def per_device(traces, source_pos, receiver_pos, aperture_list, band_index, weight_tiles):
    samples, shots, receivers = traces.shape
    rows, cols = lax.axis_size("row"), lax.axis_size("col")
    panel = band_index.shape[0]
    steps = samples // cols
    kinds, _, depth = weight_tiles.shape
    spread_len = float(panel * rows // 4)
    levels = rows // 2
    tiles, listed = aperture_list.shape
    assert receivers == 2 * shots and levels == cols

    plane_shape = (NF, 2, shots, receivers)
    half_shape = (NF, shots, receivers)
    part = pltpu.VMEM((NF, shots, 2 * receivers), BF16)
    extra = digit_rows(tiles, listed)
    table = pltpu.VMEM((receivers, panel), BF16)
    weights = pltpu.VMEM((shots, panel), F32)
    held, planes, mine, theirs, lists, places, stations, near_kinds, tiles_near = call(
        spectra_kernel,
        [
            pltpu.VMEM(traces.shape, BF16),
            pltpu.VMEM(plane_shape, BF16),
            pltpu.VMEM(half_shape, BF16),
            pltpu.VMEM((NF * shots + extra, receivers), BF16),
            pltpu.VMEM(aperture_list.shape, jnp.int32),
            pltpu.VMEM((1, shots), jnp.int32),
            pltpu.VMEM((cols, receivers), jnp.int32),
            pltpu.VMEM((1, panel), jnp.int32),
            pltpu.VMEM((kinds * steps, depth), BF16),
        ],
        [IN_HBM] * 6,
        [WHOLE] * 9,
        [
            pltpu.VMEM((2,) + half_shape, BF16),
            pltpu.VMEM((extra, DIGIT), F32),
            pltpu.SemaphoreType.DMA((PARTS + 5,)),
        ],
    )(
        *in_hbm(
            traces,
            aperture_list,
            source_pos.reshape(1, shots),
            receiver_pos.reshape(cols, receivers),
            band_index.reshape(1, panel),
            weight_tiles.reshape(kinds * steps, depth),
        )
    )
    rights = [planes] + [
        lax.ppermute(planes, "row", [(2 * a + x, 2 * b + x) for a, b in enumerate(to) for x in range(2)])
        for to in routes(levels)
    ]
    got = swap(theirs, "row", rows, 1)
    both = call(pair_kernel, pltpu.VMEM((2,) + half_shape, BF16), [WHOLE] * 2, WHOLE)(
        *in_vmem(mine, got)
    )
    left = lax.all_gather(both, "col")
    aperture, shot_weight, their_aperture, their_weight = call(
        functools.partial(tables_kernel, spread_len),
        [table, weights] * 2,
        [WHOLE] * 5,
        [WHOLE] * 4,
        [pltpu.VMEM((extra, DIGIT), F32)],
    )(*in_vmem(left, got, lists, places, stations))
    theirs, waves = call(
        functools.partial(product_kernel, levels),
        [part, pltpu.VMEM((HALF_TURN, panel), LINKT)],
        [WHOLE] * (levels + 3),
        [WHOLE] * 2,
    )(*in_vmem(left, *rights, their_aperture, their_weight))
    got_waves = swap(waves, "row", rows, 1)
    mine, columns, tiles_turned, chosen = call(
        functools.partial(own_stack_kernel, levels),
        [
            part,
            pltpu.VMEM((cols, steps, panel), F32),
            pltpu.VMEM((depth, kinds * steps), BF16),
            pltpu.VMEM((kinds, steps, panel), F32),
        ],
        [WHOLE] * (levels + 6),
        [WHOLE] * 4,
        flops=1 << 34,
    )(*in_vmem(left, *rights, held, aperture, shot_weight, near_kinds, tiles_near))
    got_part = swap(theirs, "row", rows, 1)
    band = pltpu.VMEM((steps, panel), F32)
    own, *sends = call(
        column_kernel,
        [band] + [pltpu.VMEM((steps, panel), LINKT)] * (cols - 1),
        [WHOLE] * 2,
        [WHOLE] * cols,
        [pltpu.VMEM((cols, steps, panel), F32)],
        flops=1 << 34,
    )(*in_vmem(columns, got_waves))
    order = list(range(cols - 1))[::-1]
    bands = [own] + [swap(sends[d], "col", cols, d + 1) for d in order]
    primaries, token = call(
        primaries_kernel,
        [pltpu.VMEM(traces.shape, BF16), pltpu.VMEM((8, 128), F32)],
        [WHOLE] * 3,
        [WHOLE] * 2,
        flops=1 << 20,
        moved=3 << 20,
    )(*in_vmem(mine, got_part, held))
    image = call(
        functools.partial(image_kernel, shots, cols),
        jax.ShapeDtypeStruct((depth, panel), F32),
        [WHOLE] * (cols + 3),
        WHOLE,
    )(*in_vmem(*bands, tiles_turned, chosen, token))
    return primaries, image


def solution(mesh):
    placed = (P(None, "row", "col"), P("row"), P(), P("row", None), P("row"), P())
    return jax.shard_map(
        per_device,
        mesh=mesh,
        in_specs=placed,
        out_specs=(P(None, "row", "col"), P("col", "row")),
        check_vma=False,
    )
```
